512 devices in a mesh: blk: 32 (over x, z_lo), head: 16 (over y, z_hi, core).
Axes of the slice: x: 4, y: 4, z: 16 (z_hi: 2, z_lo: 8; z = z_hi * 8 + z_lo), core: 2. Of those that a mesh axis runs over, the one named last changes fastest.
Arguments:
- query: bfloat16 [8192, 4096], P('blk', 'head'), may hold values from -6 to 6
- key: bfloat16 [8192, 256], P('blk'), may hold values from -6 to 6
- value: bfloat16 [8192, 256], P('blk'), may hold values from -6 to 6
- output: bfloat16 [8192, 4096], P('blk', 'head'), may hold values from -6 to 6
- grad_output: bfloat16 [8192, 4096], P('blk', 'head'), may hold values from -0.59765625 to 0.59765625
- log_norm: float32 [32, 8192], P('head', 'blk'), may hold values from 1 to 3
- entropy: float32 [32, 8192], P('head', 'blk'), may hold values from 0.5 to 4
- segment_ids: int32 [8192], replicated, may hold values from 0 to 15, never falling along the last dimension, each value on 1 to 2048 neighbouring positions
- weight_index: int32 [16], replicated, may hold values from 0 to 7
- penalty_weights: float32 [8], replicated, may hold values from 0.3 to 3
Outputs:
- grad_query: bfloat16 [8192, 4096], P('blk', 'head')
- grad_key: bfloat16 [8192, 256], P(('blk', 'head'))
- grad_value: bfloat16 [8192, 256], P(('blk', 'head'))
The draws below stay inside these ranges and needn't reach their ends.
Inputs may be any that keep to these rules, and one draw needn't show every extreme that they name: `segment_ids`: never falling along the window; every document has 1 to 2048 tokens, and one has exactly 2048.
All inputs are finite; a program needn't handle non-finite values.
Results may differ from the reference program's by a relative error of at most 0.0052.
Values may be sent and summed in bfloat16 or wider, within the bound.
No kernel may reach another device: no remote copies, remote signals or barrier semaphores. Data moves between devices by JAX's collectives and lax.ppermute only.
A program may use at most 64 MiB of HBM per device.

```python
import math
import jax
import jax.numpy as jnp
import numpy as np
from jax import lax

HD = 128
H = 32
KVH = 2
DOCS = 16
WEIGHTS = 8
TOKENS = 8192


def with_ends(array, own_key, smallest, top_value):
    index_at = [jax.random.randint(jax.random.fold_in(own_key, axis), (), 0, length) for axis, length in enumerate(array.shape)]
    longest = array.shape.index(max(array.shape))
    beside = index_at[:longest] + [(index_at[longest] + 1) % array.shape[longest]] + index_at[longest + 1:]
    return array.at[tuple(index_at)].set(smallest).at[tuple(beside)].set(top_value)


def levels(stream_key, dims, shards, least, largest):
    def one(position, blocks):
        steps = jax.random.uniform(jax.random.fold_in(jax.random.fold_in(stream_key, 6), position), (blocks,), jnp.float32, least / len(shards), largest / len(shards))
        return jnp.repeat(jnp.exp(steps), dims[position] // blocks).reshape((-1,) + (1,) * (len(dims) - position - 1))

    loudness = one(*shards[0])
    for cut in shards[1:]:
        loudness = loudness * one(*cut)
    return loudness


def split_up(number_of, total, limit, slope):
    weights = [(1 << 20) // math.isqrt(standing ** slope) + 1 for standing in range(2, number_of + 1)]
    rest, holding = total - limit - (number_of - 1), [1] * (number_of - 1)
    while rest > 0:
        candidates = [i for i in range(number_of - 1) if holding[i] < limit]
        mass, left = sum([weights[i] for i in candidates]), rest
        for i in candidates:
            extra = min(limit - holding[i], max(1, left * weights[i] // mass), rest)
            holding[i] = holding[i] + extra
            rest = rest - extra
    return np.array([limit] + holding)


def ragged_sizes(own_key, count, total, limit, slope):
    if count == 2:
        one = jax.random.randint(own_key, (), max(1, total - limit), min(limit, total - 1) + 1)
        return jnp.stack([one, total - one])
    tallies = jnp.asarray(split_up(count, total, limit, slope), jnp.int32)
    couples = (count - 1) // 2
    donor, receiver = tallies[1:1 + 2 * couples:2], tallies[2:2 + 2 * couples:2]
    margin = jnp.minimum(donor - 1, limit - receiver)
    moved = jax.random.randint(jax.random.fold_in(own_key, 1), (couples,), 0, 1 << 20) % (margin + 1)
    tallies = tallies.at[1:1 + 2 * couples:2].set(donor - moved).at[2:2 + 2 * couples:2].set(receiver + moved)
    return tallies[jax.random.permutation(jax.random.fold_in(own_key, 2), count)]


def noise(rng, dims, deviation, reach, pieces=(), kind=jnp.bfloat16):
    entries = jax.random.normal(rng, dims, jnp.float32) * deviation
    if len(pieces) > 0:
        entries = levels(rng, dims, pieces, -0.22, 0.18) * entries
    return jnp.clip(entries, min=-reach, max=reach).astype(kind)


def setup_inputs(seed: int = 0) -> dict:
    seeds = jax.random.split(jax.random.key(seed), 11)
    query = noise(seeds[0], (TOKENS, H * HD), 1.0, 6.0, ((0, 32), (1, 16)))
    key = noise(seeds[1], (TOKENS, KVH * HD), 1.0, 6.0, ((0, 32),))
    value = noise(seeds[2], (TOKENS, KVH * HD), 1.0, 6.0, ((0, 32),))
    output = noise(seeds[3], (TOKENS, H * HD), 1.0, 6.0, ((0, 32), (1, 16)))
    grad_output = noise(seeds[4], (TOKENS, H * HD), 0.1, 0.59765625, ((0, 32), (1, 16)))
    log_norm = jnp.clip(1.0 + 2.0 * jax.random.uniform(seeds[5], (H, TOKENS), jnp.float32) ** levels(seeds[5], (H, TOKENS), ((0, 16), (1, 32)), -0.2, 0.2), 1.0, 3.0)
    entropy = jnp.clip(0.5 + 3.5 * jax.random.uniform(seeds[6], (H, TOKENS), jnp.float32) ** levels(seeds[6], (H, TOKENS), ((0, 16), (1, 32)), -0.2, 0.2), 0.5, 4.0)
    segment_ids = jnp.searchsorted(jnp.cumsum(ragged_sizes(seeds[7], DOCS, TOKENS, TOKENS // 4, 2)), jnp.arange(TOKENS), side="right").astype(jnp.int32)
    weight_index = with_ends(jax.random.randint(seeds[8], (DOCS,), 0, WEIGHTS), jax.random.fold_in(seeds[8], 1), 0, WEIGHTS - 1).astype(jnp.int32)
    penalty_weights = jnp.clip(jnp.exp(jax.random.uniform(seeds[9], (WEIGHTS,), jnp.float32, math.log(0.3), math.log(3.0))), 0.3, 3.0)
    return dict(query=query, key=key, value=value, output=output, grad_output=grad_output, log_norm=log_norm, entropy=entropy, segment_ids=segment_ids, weight_index=weight_index, penalty_weights=penalty_weights)


def reference(query, key, value, output, grad_output, log_norm, entropy, segment_ids, weight_index, penalty_weights):
    score_scale = HD ** -0.5
    heads_shared = H // KVH
    span_rows = math.gcd(TOKENS, 1024)
    doc_rate = penalty_weights[weight_index]
    row_rate = doc_rate[segment_ids]
    positions = jnp.arange(TOKENS, dtype=jnp.int32)

    def one_head(head_index):
        kv_index = head_index // heads_shared
        q_cols = lax.dynamic_slice_in_dim(query, (head_index * HD).astype(jnp.int32), HD, 1)
        do_cols = lax.dynamic_slice_in_dim(grad_output, (head_index * HD).astype(jnp.int32), HD, 1)
        o_cols = lax.dynamic_slice_in_dim(output, (head_index * HD).astype(jnp.int32), HD, 1)
        k_cols = lax.dynamic_slice_in_dim(key, (kv_index * HD).astype(jnp.int32), HD, 1)
        v_cols = lax.dynamic_slice_in_dim(value, (kv_index * HD).astype(jnp.int32), HD, 1)
        lse_row = lax.dynamic_index_in_dim(log_norm, head_index, 0, keepdims=False)
        ent_row = lax.dynamic_index_in_dim(entropy, head_index, 0, keepdims=False)
        row_delta = jnp.sum(do_cols.astype(jnp.float32) * o_cols.astype(jnp.float32), 1)

        def block(carry, block_index):
            key_acc, value_acc = carry
            first = (block_index * span_rows).astype(jnp.int32)
            q_block = lax.dynamic_slice_in_dim(q_cols, first, span_rows, 0)
            do_block = lax.dynamic_slice_in_dim(do_cols, first, span_rows, 0)
            seg_block = lax.dynamic_slice_in_dim(segment_ids, first, span_rows, 0)
            pos_block = lax.dynamic_slice_in_dim(positions, first, span_rows, 0)
            lse_block = lax.dynamic_slice_in_dim(lse_row, first, span_rows, 0)[:, None]
            ent_block = lax.dynamic_slice_in_dim(ent_row, first, span_rows, 0)[:, None]
            delta_block = lax.dynamic_slice_in_dim(row_delta, first, span_rows, 0)[:, None]
            rate_block = lax.dynamic_slice_in_dim(row_rate, first, span_rows, 0)[:, None]
            scores = jnp.dot(q_block, k_cols.T, preferred_element_type=jnp.float32) * score_scale
            visible = (seg_block[:, None] == segment_ids[None, :]) & (positions[None, :] <= pos_block[:, None])
            probs = jnp.where(visible, jnp.exp(scores - lse_block), 0.0)
            dprobs = jnp.dot(do_block, v_cols.T, preferred_element_type=jnp.float32)
            dscores = probs * (dprobs - delta_block - rate_block * (scores - lse_block + ent_block))
            probs_low = probs.astype(jnp.bfloat16)
            dscores_low = dscores.astype(jnp.bfloat16)
            query_rows = jnp.dot(dscores_low, k_cols, preferred_element_type=jnp.float32)
            key_acc = key_acc + jnp.dot(dscores_low.T, q_block, preferred_element_type=jnp.float32)
            value_acc = value_acc + jnp.dot(probs_low.T, do_block, preferred_element_type=jnp.float32)
            return (key_acc, value_acc), query_rows

        zeros = jnp.zeros((TOKENS, HD), jnp.float32)
        (key_acc, value_acc), query_grad = lax.scan(block, (zeros, zeros), jnp.arange(TOKENS // span_rows, dtype=jnp.int32))
        query_grad = (query_grad.reshape(TOKENS, HD) * score_scale).astype(jnp.bfloat16)
        return query_grad, key_acc, value_acc

    def one_shared(kv_index):
        def add_head(carry, head_index):
            query_grad, key_acc, value_acc = one_head(head_index)
            return (carry[0] + key_acc, carry[1] + value_acc), query_grad

        zeros = jnp.zeros((TOKENS, HD), jnp.float32)
        members = kv_index * heads_shared + jnp.arange(heads_shared, dtype=jnp.int32)
        (key_sum, value_sum), query_grad = lax.scan(add_head, (zeros, zeros), members)
        return query_grad, (key_sum * score_scale).astype(jnp.bfloat16), value_sum.astype(jnp.bfloat16)

    query_grad, key_sum, value_sum = lax.map(one_shared, jnp.arange(KVH, dtype=jnp.int32))
    grad_query = query_grad.reshape(H, TOKENS, HD).transpose(1, 0, 2).reshape(TOKENS, H * HD)
    grad_key = key_sum.transpose(1, 0, 2).reshape(TOKENS, KVH * HD)
    grad_value = value_sum.transpose(1, 0, 2).reshape(TOKENS, KVH * HD)
    return grad_query, grad_key, grad_value
```

```python
import functools
import math

import jax
import jax.numpy as jnp
from jax import lax
from jax.experimental import pallas as pl
from jax.experimental.pallas import tpu as pltpu
from jax.sharding import PartitionSpec as P

HD = 128
ROWS = 256
SCALE = HD ** (-0.5)
LOG2E = math.log2(math.e)
MSG = 4 * ROWS + 32
GROUP = 8
F32 = jnp.float32
BF16 = jnp.bfloat16
VMEM_LIMIT = 48 * 1024 * 1024

FIRST = ((1, 7), (2, 6))
SECOND = ((3, 5), (4, 8))


def place(index):
    blk, head = divmod(index, 16)
    x, z_lo = divmod(blk, 8)
    y, rest = divmod(head, 4)
    z_hi, core = divmod(rest, 2)
    return x, y, z_hi * 8 + z_lo, core


def device(x, y, z, core):
    z_hi, z_lo = divmod(z % 16, 8)
    return ((x % 4) * 8 + z_lo) * 16 + (y % 4) * 4 + z_hi * 2 + core


def pairs_from(source_of):
    return [(source_of(index), index) for index in range(512)]


def back_source(table, index):
    x, y, z, core = place(index)
    steps = table[y % 2][core]
    source_x = x if z % 8 >= steps else x - 1
    up = steps < 4 or (steps == 4 and z % 2 == 0)
    return device(source_x, y, z - steps if up else z + 8 - steps, core)


def other_core(index):
    x, y, z, core = place(index)
    return device(x, y, z, 1 - core)


def other_y(index):
    x, y, z, core = place(index)
    return device(x, y ^ 1, z, core)


def inverse(pairs):
    return [(target, source) for source, target in pairs]


def moved(value, pairs):
    return lax.ppermute(value, ("blk", "head"), pairs)


def steps_here(table):
    head = lax.axis_index("head")
    odd = lax.rem(lax.div(head, 4), 2) == 1
    core = lax.rem(head, 2) == 1
    return jnp.where(
        odd,
        jnp.where(core, table[1][1], table[1][0]),
        jnp.where(core, table[0][1], table[0][0]),
    )


def nt(a, b):
    return lax.dot_general(a, b, (((1,), (1,)), ((), ())), preferred_element_type=F32)


def nn(a, b):
    return lax.dot_general(a, b, (((1,), (0,)), ((), ())), preferred_element_type=F32)


def transposed(block):
    return block.astype(F32).T.astype(BF16)


def prep_kernel(
    q, k, v, o, do, lse, ent, seg, weight_index, weights, msg, kv, aux, rows
):
    blk = lax.axis_index("blk")
    head = lax.axis_index("head")
    column = pl.multiple_of(lax.div(head, 8) * HD, HD)
    kv[:, :HD] = k[:, pl.ds(column, HD)]
    kv[:, HD:] = v[:, pl.ds(column, HD)]
    docs = weight_index.shape[0]
    tokens = seg[...]
    first = seg[pl.ds(2 * blk, 1), :]
    second = seg[pl.ds(2 * blk + 1, 1), :]
    seg_rows = jnp.concatenate([first, second], axis=1)
    rate = jnp.zeros((1, ROWS), F32)
    for d in range(docs):
        rows[d : d + 1, :HD] = jnp.sum(
            jnp.where(tokens < d, 1.0, 0.0), axis=0, keepdims=True
        )
        rate = jnp.where(seg_rows == d, weights[weight_index[d]], rate)
    starts = jnp.sum(rows[:, :HD], axis=1, keepdims=True)
    doc = lax.broadcasted_iota(jnp.int32, (docs, ROWS), 0)
    start = jnp.sum(jnp.where(doc == seg_rows, starts, 0.0), axis=0, keepdims=True)
    aux[...] = jnp.zeros_like(aux)
    aux[0:1, :] = start
    aux[1:2, :] = rate
    rows[...] = jnp.zeros_like(rows)
    for h in range(2):
        columns = slice(h * HD, (h + 1) * HD)
        do_h = do[:, columns]
        msg[h * 512 : h * 512 + ROWS, :] = q[:, columns]
        msg[h * 512 + ROWS : h * 512 + 512, :] = do_h
        product = do_h.astype(F32) * o[:, columns].astype(F32)
        delta = jnp.sum(product.T, axis=0, keepdims=True)
        lse_h = lse[h : h + 1, :]
        const = delta + rate * (ent[h : h + 1, :] - lse_h)
        for at, value in ((3 * h, lse_h), (6 + 3 * h, const)):
            for part in range(3):
                piece = value.astype(BF16).astype(F32)
                rows[at + part : at + part + 1, :] = piece
                value = value - piece
    msg[1024:1040, :] = rows[:, :HD].astype(BF16)
    msg[1040:1056, :] = rows[:, HD:].astype(BF16)


def prep(q, k, v, o, do, lse, ent, seg, weight_index, weights):
    vmem = pl.BlockSpec(memory_space=pltpu.VMEM)
    smem = pl.BlockSpec(memory_space=pltpu.SMEM)
    return pl.pallas_call(
        prep_kernel,
        out_shape=(
            jax.ShapeDtypeStruct((MSG, HD), BF16),
            jax.ShapeDtypeStruct((ROWS, 2 * HD), BF16),
            jax.ShapeDtypeStruct((8, ROWS), F32),
        ),
        in_specs=[vmem] * 8 + [smem] * 2,
        out_specs=(vmem,) * 3,
        scratch_shapes=[pltpu.VMEM((16, ROWS), F32)],
        name="prep",
        compiler_params=pltpu.CompilerParams(vmem_limit_bytes=VMEM_LIMIT),
    )(q, k, v, o, do, lse, ent, seg, weight_index, weights)


def row_terms(stats_lo, stats_hi, h):
    def whole(at):
        both = [
            half[at : at + 1, :] + half[at + 1 : at + 2, :] + half[at + 2 : at + 3, :]
            for half in (stats_lo, stats_hi)
        ]
        return jnp.concatenate(both, axis=1)

    return whole(3 * h) * LOG2E, whole(6 + 3 * h)


def unit(key_block, key_turned, value_block, q, do, lse2, const, rate, visible):
    scores = nt(key_block, q)
    probs = jnp.where(visible, jnp.exp2(scores * (SCALE * LOG2E) - lse2), 0.0)
    dprobs = nt(value_block, do)
    dscores = probs * (dprobs - const - scores * rate)
    probs_low = probs.astype(BF16)
    dscores_low = dscores.astype(BF16)
    return nn(key_turned, dscores_low), nn(dscores_low, q), nn(probs_low, do)


def diag_kernel(msg, kv, aux, dq, dkv):
    blk = lax.axis_index("blk")
    threshold = aux[0:1, :] - (blk * ROWS).astype(F32)
    rate = aux[1:2, :] * SCALE
    key_at = lax.broadcasted_iota(jnp.int32, (ROWS, ROWS), 0)
    query_at = lax.broadcasted_iota(jnp.int32, (ROWS, ROWS), 1)
    visible = (key_at <= query_at) & (key_at.astype(F32) >= threshold)
    key_block, value_block = kv[:, :HD], kv[:, HD:]
    key_turned = transposed(key_block)
    stats_lo = msg[1024:1040, :].astype(F32)
    stats_hi = msg[1040:1056, :].astype(F32)
    key_sum = value_sum = None
    for h in range(2):
        lse2, const = row_terms(stats_lo, stats_hi, h)
        q = msg[h * 512 : h * 512 + ROWS, :]
        do = msg[h * 512 + ROWS : h * 512 + 512, :]
        query_add, key_add, value_add = unit(
            key_block, key_turned, value_block, q, do, lse2, const, rate, visible
        )
        dq[h] = query_add
        key_sum = key_add if h == 0 else key_sum + key_add
        value_sum = value_add if h == 0 else value_sum + value_add
    dkv[:, :HD] = key_sum
    dkv[:, HD:] = value_sum


def diag(msg, kv, aux):
    vmem = pl.BlockSpec(memory_space=pltpu.VMEM)
    return pl.pallas_call(
        diag_kernel,
        out_shape=(
            jax.ShapeDtypeStruct((2, HD, ROWS), F32),
            jax.ShapeDtypeStruct((ROWS, 2 * HD), F32),
        ),
        in_specs=[vmem] * 3,
        out_specs=(vmem,) * 2,
        name="diag",
        compiler_params=pltpu.CompilerParams(vmem_limit_bytes=VMEM_LIMIT),
        cost_estimate=pl.CostEstimate(
            flops=20 * ROWS * ROWS * HD, bytes_accessed=1 << 20, transcendentals=2 * ROWS * ROWS
        ),
    )(msg, kv, aux)


def main_kernel(
    own, other, kv_a, kv_b, aux, dq_diag, dkv_a, dkv_b, dq_send, dq_keep, dq, dkv
):
    blk = lax.axis_index("blk")
    start = aux[0:1, :]
    rate = aux[1:2, :] * SCALE
    first_start = jnp.min(start)
    key_at = lax.broadcasted_iota(jnp.int32, (ROWS, ROWS), 0).astype(F32)
    dq[...] = jnp.zeros_like(dq)
    dq[0, 0] = dq_diag[0]
    dq[0, 1] = dq_diag[1]
    for kv, table, out in ((kv_a, FIRST, dkv_a), (kv_b, SECOND, dkv_b)):
        key_start = ((blk - steps_here(table)) * ROWS).astype(F32)
        seen = key_start + (ROWS - 1) >= first_start

        @pl.when(jnp.logical_not(seen))
        def _():
            out[...] = jnp.zeros_like(out)

        @pl.when(seen)
        def _():
            key_block, value_block = kv[:, :HD], kv[:, HD:]
            key_turned = transposed(key_block)
            threshold = start - key_start
            dkv[...] = jnp.zeros_like(dkv)

            @pl.loop(0, 2)
            def _(src):
                base = src * MSG
                for part, ref in ((0, own), (1, other)):
                    at = pl.multiple_of(base + 1024, 16)
                    stats_lo = ref[pl.ds(at, 16), :].astype(F32)
                    stats_hi = ref[pl.ds(at + 16, 16), :].astype(F32)
                    for h in range(2):
                        lse2, const = row_terms(stats_lo, stats_hi, h)
                        at = pl.multiple_of(base + h * 512, 16)
                        q = ref[pl.ds(at, ROWS), :]
                        do = ref[pl.ds(at + ROWS, ROWS), :]
                        visible = key_at >= threshold
                        query_add, key_add, value_add = unit(
                            key_block,
                            key_turned,
                            value_block,
                            q,
                            do,
                            lse2,
                            const,
                            rate,
                            visible,
                        )
                        dq[part, 2 * src + h] += query_add
                        dkv[:, :HD] += key_add
                        dkv[:, HD:] += value_add

            out[...] = dkv[...].astype(BF16)

    for n in range(4):
        dq_keep[n * ROWS : (n + 1) * ROWS, :] = dq[0, n].T
        dq_send[n * ROWS : (n + 1) * ROWS, :] = dq[1, n].T.astype(BF16)


def main(own, other, kv_a, kv_b, aux, dq_diag):
    vmem = pl.BlockSpec(memory_space=pltpu.VMEM)
    return pl.pallas_call(
        main_kernel,
        out_shape=(
            jax.ShapeDtypeStruct((ROWS, 2 * HD), BF16),
            jax.ShapeDtypeStruct((ROWS, 2 * HD), BF16),
            jax.ShapeDtypeStruct((4 * ROWS, HD), BF16),
            jax.ShapeDtypeStruct((4 * ROWS, HD), F32),
        ),
        in_specs=[vmem] * 6,
        out_specs=(vmem,) * 4,
        scratch_shapes=[
            pltpu.VMEM((2, 4, HD, ROWS), F32),
            pltpu.VMEM((ROWS, 2 * HD), F32),
        ],
        name="main",
        compiler_params=pltpu.CompilerParams(vmem_limit_bytes=VMEM_LIMIT),
        cost_estimate=pl.CostEstimate(
            flops=160 * ROWS * ROWS * HD, bytes_accessed=3 << 20, transcendentals=16 * ROWS * ROWS
        ),
    )(own, other, kv_a, kv_b, aux, dq_diag)


def last_kernel(terms, dq_keep, dq_core, dq_y, grad_query, grad_key, grad_value):
    for h in range(2):
        at = slice(h * ROWS, (h + 1) * ROWS)
        total = dq_keep[at, :] + dq_core[at, :].astype(F32) + dq_y[at, :].astype(F32)
        grad_query[:, h * HD : (h + 1) * HD] = (total * SCALE).astype(BF16)
    half = terms.shape[0] // 2
    for g in range(2):
        total = jnp.sum(terms[g * half : (g + 1) * half], axis=0)
        grad_key[:, g * HD : (g + 1) * HD] = (total[:, :HD] * SCALE).astype(BF16)
        grad_value[:, g * HD : (g + 1) * HD] = total[:, HD:].astype(BF16)


def last(terms, dq_keep, dq_core, dq_y):
    vmem = pl.BlockSpec(memory_space=pltpu.VMEM)
    rows = terms.shape[1]
    return pl.pallas_call(
        last_kernel,
        out_shape=(
            jax.ShapeDtypeStruct((ROWS, 2 * HD), BF16),
            jax.ShapeDtypeStruct((rows, 2 * HD), BF16),
            jax.ShapeDtypeStruct((rows, 2 * HD), BF16),
        ),
        in_specs=[vmem] * 4,
        out_specs=(vmem,) * 3,
        name="last",
        compiler_params=pltpu.CompilerParams(vmem_limit_bytes=VMEM_LIMIT),
    )(terms, dq_keep, dq_core, dq_y)


def local(
    query,
    key,
    value,
    output,
    grad_output,
    log_norm,
    entropy,
    segment_ids,
    weight_index,
    penalty_weights,
):
    to_core = pairs_from(other_core)
    to_y = pairs_from(other_y)
    back_a = pairs_from(functools.partial(back_source, FIRST))
    back_b = pairs_from(functools.partial(back_source, SECOND))
    msg, kv, aux = prep(
        query,
        key,
        value,
        output,
        grad_output,
        log_norm,
        entropy,
        segment_ids.reshape(-1, HD),
        weight_index,
        penalty_weights,
    )
    msg_y = moved(msg, to_y)
    kv_a = moved(kv, back_a)
    kv_b = moved(kv, back_b)
    dq_diag, dkv_diag = diag(msg, kv, aux)
    msg_y, kv_a = lax.optimization_barrier((msg_y, kv_a))
    own = jnp.concatenate([msg, msg_y], axis=0)
    other = moved(own, to_core)
    dkv_a, dkv_b, dq_send, dq_keep = main(own, other, kv_a, kv_b, aux, dq_diag)
    got_a = moved(dkv_a, inverse(back_a))
    got_b = moved(dkv_b, inverse(back_b))
    dq_core = moved(dq_send, to_core)
    dq_pass = (dq_keep[512:] + dq_core[512:].astype(F32)).astype(BF16)
    dq_y = moved(dq_pass, to_y)
    terms = dkv_diag + got_a.astype(F32) + got_b.astype(F32)
    terms = lax.all_to_all(terms.reshape(16, 16, 2 * HD), "head", 0, 0)
    return last(terms, dq_keep, dq_core, dq_y)


def solution(mesh):
    in_specs = (
        P("blk", "head"),
        P("blk", None),
        P("blk", None),
        P("blk", "head"),
        P("blk", "head"),
        P("head", "blk"),
        P("head", "blk"),
        P(),
        P(),
        P(),
    )
    out_specs = (P("blk", "head"), P(("blk", "head"), None), P(("blk", "head"), None))
    return jax.shard_map(local, mesh=mesh, in_specs=in_specs, out_specs=out_specs, check_vma=False)
```

```python
import functools
import math

import jax
import jax.numpy as jnp
from jax import lax
from jax.experimental import pallas as pl
from jax.experimental.pallas import tpu as pltpu
from jax.sharding import PartitionSpec as P

HD = 128
ROWS = 256
SCALE = HD ** (-0.5)
LOG2E = math.log2(math.e)
MSG = 4 * ROWS + 64
GROUP = 8
F32 = jnp.float32
BF16 = jnp.bfloat16
PREP_VMEM_LIMIT = 62 * 1024 * 1024
VMEM_LIMIT = 24 * 1024 * 1024

FIRST = ((1, 7), (2, 6))
SECOND = ((3, 5), (4, 8))


def place(index):
    blk, head = divmod(index, 16)
    x, z_lo = divmod(blk, 8)
    y, rest = divmod(head, 4)
    z_hi, core = divmod(rest, 2)
    return x, y, z_hi * 8 + z_lo, core


def device(x, y, z, core):
    z_hi, z_lo = divmod(z % 16, 8)
    return ((x % 4) * 8 + z_lo) * 16 + (y % 4) * 4 + z_hi * 2 + core


def pairs_from(source_of):
    return [(source_of(index), index) for index in range(512)]


def back_source(table, index):
    x, y, z, core = place(index)
    steps = table[y % 2][core]
    source_x = x if z % 8 >= steps else x - 1
    up = steps < 4 or (steps == 4 and z % 2 == 0)
    return device(source_x, y, z - steps if up else z + 8 - steps, core)


def other_core(index):
    x, y, z, core = place(index)
    return device(x, y, z, 1 - core)


def other_y(index):
    x, y, z, core = place(index)
    return device(x, y ^ 1, z, core)


def inverse(pairs):
    return [(target, source) for source, target in pairs]


def moved(value, pairs):
    return lax.ppermute(value, ("blk", "head"), pairs)


def steps_here(table):
    head = lax.axis_index("head")
    odd = lax.rem(lax.div(head, 4), 2) == 1
    core = lax.rem(head, 2) == 1
    return jnp.where(
        odd,
        jnp.where(core, table[1][1], table[1][0]),
        jnp.where(core, table[0][1], table[0][0]),
    )


def nt(a, b):
    return lax.dot_general(a, b, (((1,), (1,)), ((), ())), preferred_element_type=F32)


def nn(a, b):
    return lax.dot_general(a, b, (((1,), (0,)), ((), ())), preferred_element_type=F32)


def transposed(block):
    return block.astype(F32).T.astype(BF16)


def prep_kernel(
    q_in,
    k_in,
    v_in,
    o_in,
    do_in,
    lse_in,
    ent_in,
    seg_in,
    weight_index_in,
    weights_in,
    msg,
    kv,
    aux,
    q,
    k,
    v,
    o,
    do,
    lse,
    ent,
    seg,
    weight_index,
    weights,
    rows,
    sems,
):
    arriving = [
        pltpu.make_async_copy(source, target, sems.at[n])
        for n, (source, target) in enumerate(
            (
                (weight_index_in, weight_index),
                (weights_in, weights),
                (seg_in, seg),
                (lse_in, lse),
                (ent_in, ent),
                (do_in, do),
                (o_in, o),
                (q_in, q),
                (k_in, k),
                (v_in, v),
            )
        )
    ]
    for copy in arriving:
        copy.start()
    for copy in arriving:
        copy.wait()
    blk = lax.axis_index("blk")
    head = lax.axis_index("head")
    column = pl.multiple_of(lax.div(head, 8) * HD, HD)
    kv[:, :HD] = k[:, pl.ds(column, HD)]
    kv[:, HD:] = v[:, pl.ds(column, HD)]
    docs = weight_index.shape[0]
    tokens = seg[...]
    first = seg[pl.ds(2 * blk, 1), :]
    second = seg[pl.ds(2 * blk + 1, 1), :]
    seg_rows = jnp.concatenate([first, second], axis=1)
    rate = jnp.zeros((1, ROWS), F32)
    for d in range(docs):
        rows[d : d + 1, :HD] = jnp.sum(
            jnp.where(tokens < d, 1.0, 0.0), axis=0, keepdims=True
        )
        rate = jnp.where(seg_rows == d, weights[weight_index[d]], rate)
    starts = jnp.sum(rows[:docs, :HD], axis=1, keepdims=True)
    doc = lax.broadcasted_iota(jnp.int32, (docs, ROWS), 0)
    start = jnp.sum(jnp.where(doc == seg_rows, starts, 0.0), axis=0, keepdims=True)
    aux[...] = jnp.zeros_like(aux)
    aux[0:1, :] = start
    aux[1:2, :] = rate
    rows[...] = jnp.zeros_like(rows)
    for h in range(2):
        columns = slice(h * HD, (h + 1) * HD)
        do_h = do[:, columns]
        msg[h * 512 : h * 512 + ROWS, :] = q[:, columns]
        msg[h * 512 + ROWS : h * 512 + 512, :] = do_h
        product = do_h.astype(F32) * o[:, columns].astype(F32)
        delta = jnp.sum(product.T, axis=0, keepdims=True)
        lse_h = lse[h : h + 1, :]
        const = delta + rate * (ent[h : h + 1, :] - lse_h)
        for at, value in ((0, lse_h), (3, const)):
            for part in range(3):
                piece = value.astype(BF16).astype(F32)
                rows[at + part : at + part + 1, :] = piece
                value = value - piece
        at = 1024 + 32 * h
        msg[at : at + 16, :] = rows[:, :HD].astype(BF16)
        msg[at + 16 : at + 32, :] = rows[:, HD:].astype(BF16)


def prep(*arrays):
    vmem = pl.BlockSpec(memory_space=pltpu.VMEM)
    held = [pltpu.VMEM(array.shape, array.dtype) for array in arrays[:8]]
    held += [pltpu.SMEM(array.shape, array.dtype) for array in arrays[8:]]
    return pl.pallas_call(
        prep_kernel,
        out_shape=(
            jax.ShapeDtypeStruct((MSG, HD), BF16),
            jax.ShapeDtypeStruct((ROWS, 2 * HD), BF16),
            jax.ShapeDtypeStruct((8, ROWS), F32),
        ),
        in_specs=[pl.BlockSpec(memory_space=pltpu.HBM)] * 10,
        out_specs=(vmem,) * 3,
        scratch_shapes=held
        + [pltpu.VMEM((16, ROWS), F32), pltpu.SemaphoreType.DMA((10,))],
        name="prep",
        compiler_params=pltpu.CompilerParams(vmem_limit_bytes=PREP_VMEM_LIMIT),
    )(*arrays)


def row_terms(ref, h):
    at = 1024 + 32 * h
    if not isinstance(h, int):
        at = pl.multiple_of(at, 16)
    halves = [ref[pl.ds(at, 16), :].astype(F32), ref[pl.ds(at + 16, 16), :].astype(F32)]

    def whole(row):
        both = [
            half[row : row + 1, :] + half[row + 1 : row + 2, :] + half[row + 2 : row + 3, :]
            for half in halves
        ]
        return jnp.concatenate(both, axis=1)

    return whole(0) * LOG2E, whole(3)


def unit(key_block, key_turned, value_block, q, do, lse2, const, rate, visible):
    scores = nt(key_block, q)
    probs = jnp.where(visible, jnp.exp2(scores * (SCALE * LOG2E) - lse2), 0.0)
    dprobs = nt(value_block, do)
    dscores = probs * (dprobs - const - scores * rate)
    probs_low = probs.astype(BF16)
    dscores_low = dscores.astype(BF16)
    return nn(key_turned, dscores_low), nn(dscores_low, q), nn(probs_low, do)


def diag_kernel(msg, kv, aux, dq, dkv):
    blk = lax.axis_index("blk")
    threshold = aux[0:1, :] - (blk * ROWS).astype(F32)
    rate = aux[1:2, :] * SCALE
    key_at = lax.broadcasted_iota(jnp.int32, (ROWS, ROWS), 0)
    query_at = lax.broadcasted_iota(jnp.int32, (ROWS, ROWS), 1)
    visible = (key_at <= query_at) & (key_at.astype(F32) >= threshold)
    key_block, value_block = kv[:, :HD], kv[:, HD:]
    key_turned = transposed(key_block)
    key_sum = value_sum = None
    for h in range(2):
        lse2, const = row_terms(msg, h)
        q = msg[h * 512 : h * 512 + ROWS, :]
        do = msg[h * 512 + ROWS : h * 512 + 512, :]
        query_add, key_add, value_add = unit(
            key_block, key_turned, value_block, q, do, lse2, const, rate, visible
        )
        dq[h] = query_add
        key_sum = key_add if h == 0 else key_sum + key_add
        value_sum = value_add if h == 0 else value_sum + value_add
    dkv[:, :HD] = key_sum
    dkv[:, HD:] = value_sum


def diag(msg, kv, aux):
    vmem = pl.BlockSpec(memory_space=pltpu.VMEM)
    return pl.pallas_call(
        diag_kernel,
        out_shape=(
            jax.ShapeDtypeStruct((2, HD, ROWS), F32),
            jax.ShapeDtypeStruct((ROWS, 2 * HD), F32),
        ),
        in_specs=[vmem] * 3,
        out_specs=(vmem,) * 2,
        name="diag",
        compiler_params=pltpu.CompilerParams(vmem_limit_bytes=VMEM_LIMIT),
        cost_estimate=pl.CostEstimate(
            flops=20 * ROWS * ROWS * HD, bytes_accessed=1 << 20, transcendentals=2 * ROWS * ROWS
        ),
    )(msg, kv, aux)


def block_kernel(table, last_block, own, core, y, cross, kv, aux, dq_in, *rest):
    if last_block:
        out, dq_send, dq_keep, dq, dkv = rest
    else:
        out, dq, dkv = rest
    blk = lax.axis_index("blk")
    start = aux[0:1, :]
    rate = aux[1:2, :] * SCALE
    key_start = ((blk - steps_here(table)) * ROWS).astype(F32)
    seen = key_start + (ROWS - 1) >= jnp.min(start)
    if last_block:
        dq[...] = dq_in[...]
    else:
        dq[...] = jnp.zeros_like(dq)
        dq[0] = dq_in[...]
    dkv[...] = jnp.zeros_like(dkv)

    @pl.when(seen)
    def _():
        key_block, value_block = kv[:, :HD], kv[:, HD:]
        key_turned = transposed(key_block)
        threshold = start - key_start
        key_at = lax.broadcasted_iota(jnp.int32, (ROWS, ROWS), 0).astype(F32)

        @pl.loop(0, 2)
        def _(h):
            for n, ref in enumerate((own, core, y, cross)):
                lse2, const = row_terms(ref, h)
                at = pl.multiple_of(h * 512, 512)
                q = ref[pl.ds(at, ROWS), :]
                do = ref[pl.ds(at + ROWS, ROWS), :]
                query_add, key_add, value_add = unit(
                    key_block,
                    key_turned,
                    value_block,
                    q,
                    do,
                    lse2,
                    const,
                    rate,
                    key_at >= threshold,
                )
                dq[n, h] += query_add
                dkv[:, :HD] += key_add
                dkv[:, HD:] += value_add

    out[...] = dkv[...].astype(BF16)
    if last_block:
        for n, (kept, sent) in enumerate(((0, 1), (2, 3))):
            for h in range(2):
                at = slice((2 * n + h) * ROWS, (2 * n + h + 1) * ROWS)
                dq_keep[at, :] = dq[kept, h].T
                dq_send[at, :] = dq[sent, h].T.astype(BF16)


def block(table, last_block, own, core, y, cross, kv, aux, dq_in):
    vmem = pl.BlockSpec(memory_space=pltpu.VMEM)
    sums = (4, 2, HD, ROWS)
    out_shape = [jax.ShapeDtypeStruct((ROWS, 2 * HD), BF16)]
    scratch = [pltpu.VMEM((ROWS, 2 * HD), F32)]
    if last_block:
        out_shape.append(jax.ShapeDtypeStruct((4 * ROWS, HD), BF16))
        out_shape.append(jax.ShapeDtypeStruct((4 * ROWS, HD), F32))
        scratch.insert(0, pltpu.VMEM(sums, F32))
    else:
        out_shape.append(jax.ShapeDtypeStruct(sums, F32))
    return pl.pallas_call(
        functools.partial(block_kernel, table, last_block),
        out_shape=tuple(out_shape),
        in_specs=[vmem] * 7,
        out_specs=(vmem,) * len(out_shape),
        scratch_shapes=scratch,
        name="second" if last_block else "first",
        compiler_params=pltpu.CompilerParams(vmem_limit_bytes=VMEM_LIMIT),
        cost_estimate=pl.CostEstimate(
            flops=80 * ROWS * ROWS * HD, bytes_accessed=3 << 20, transcendentals=8 * ROWS * ROWS
        ),
    )(own, core, y, cross, kv, aux, dq_in)


def last_kernel(terms, dq_keep, dq_core, dq_y, grad_query, grad_key, grad_value):
    for h in range(2):
        at = slice(h * ROWS, (h + 1) * ROWS)
        total = dq_keep[at, :] + dq_core[at, :].astype(F32) + dq_y[at, :].astype(F32)
        grad_query[:, h * HD : (h + 1) * HD] = (total * SCALE).astype(BF16)
    half = terms.shape[0] // 2
    for g in range(2):
        total = jnp.sum(terms[g * half : (g + 1) * half].astype(F32), axis=0)
        grad_key[:, g * HD : (g + 1) * HD] = (total[:, :HD] * SCALE).astype(BF16)
        grad_value[:, g * HD : (g + 1) * HD] = total[:, HD:].astype(BF16)


def last(terms, dq_keep, dq_core, dq_y):
    vmem = pl.BlockSpec(memory_space=pltpu.VMEM)
    rows = terms.shape[1]
    return pl.pallas_call(
        last_kernel,
        out_shape=(
            jax.ShapeDtypeStruct((ROWS, 2 * HD), BF16),
            jax.ShapeDtypeStruct((rows, 2 * HD), BF16),
            jax.ShapeDtypeStruct((rows, 2 * HD), BF16),
        ),
        in_specs=[vmem] * 4,
        out_specs=(vmem,) * 3,
        name="last",
        compiler_params=pltpu.CompilerParams(vmem_limit_bytes=VMEM_LIMIT),
    )(terms, dq_keep, dq_core, dq_y)


def local(
    query,
    key,
    value,
    output,
    grad_output,
    log_norm,
    entropy,
    segment_ids,
    weight_index,
    penalty_weights,
):
    to_core = pairs_from(other_core)
    to_y = pairs_from(other_y)
    to_cross = pairs_from(lambda index: other_y(other_core(index)))
    back_a = pairs_from(functools.partial(back_source, FIRST))
    back_b = pairs_from(functools.partial(back_source, SECOND))
    msg, kv, aux = prep(
        query,
        key,
        value,
        output,
        grad_output,
        log_norm,
        entropy,
        segment_ids.reshape(-1, HD),
        weight_index,
        penalty_weights,
    )
    msg_y = moved(msg, to_y)
    msg_cross = moved(msg, to_cross)
    kv_a = moved(kv, back_a)
    kv_b = moved(kv, back_b)
    msg_core = moved(msg, to_core)
    dq_diag, dkv_diag = diag(msg, kv, aux)
    messages = (msg, msg_core, msg_y, msg_cross)
    dkv_a, dq = block(FIRST, False, *messages, kv_a, aux, dq_diag)
    got_a = moved(dkv_a, inverse(back_a))
    dkv_b, dq_send, dq_keep = block(SECOND, True, *messages, kv_b, aux, dq)
    got_b = moved(dkv_b, inverse(back_b))
    dq_core = moved(dq_send, to_core)
    dq_pass = (dq_keep[512:] + dq_core[512:].astype(F32)).astype(BF16)
    terms = (dkv_diag + got_a.astype(F32) + got_b.astype(F32)).astype(BF16)
    dq_y = moved(dq_pass, to_y)
    terms = lax.all_to_all(terms.reshape(16, 16, 2 * HD), "head", 0, 0)
    return last(terms, dq_keep, dq_core, dq_y)


def solution(mesh):
    in_specs = (
        P("blk", "head"),
        P("blk", None),
        P("blk", None),
        P("blk", "head"),
        P("blk", "head"),
        P("head", "blk"),
        P("head", "blk"),
        P(),
        P(),
        P(),
    )
    out_specs = (P("blk", "head"), P(("blk", "head"), None), P(("blk", "head"), None))
    return jax.shard_map(local, mesh=mesh, in_specs=in_specs, out_specs=out_specs, check_vma=False)
```

```python
import functools
import math

import jax
import jax.numpy as jnp
from jax import lax
from jax.experimental import pallas as pl
from jax.experimental.pallas import tpu as pltpu
from jax.sharding import PartitionSpec as P

HD = 128
ROWS = 256
SCALE = HD ** (-0.5)
LOG2E = math.log2(math.e)
MSG = 4 * ROWS + 64
GROUP = 8
F32 = jnp.float32
OWN_FLOPS = 1 << 28
EARLY_FLOPS = 1 << 34
LATE_FLOPS = 1 << 30
TURN_FLOPS = 1 << 27
QUERY_FLOPS = 1 << 34
BF16 = jnp.bfloat16
PREP_VMEM_LIMIT = 62 * 1024 * 1024
VMEM_LIMIT = 24 * 1024 * 1024

NEAR = ((1, 7), (2, 6))
FAR = ((3, 5), (4, 8))

HEAD_ORDER = [y * 4 + z_hi * 2 + core for z_hi in (1, 0) for y in range(4) for core in range(2)]


def place(index):
    blk, head = divmod(index, 16)
    x, z_lo = divmod(blk, 8)
    y, rest = divmod(head, 4)
    z_hi, core = divmod(rest, 2)
    return x, y, z_hi * 8 + z_lo, core


def device(x, y, z, core):
    z_hi, z_lo = divmod(z % 16, 8)
    return ((x % 4) * 8 + z_lo) * 16 + (y % 4) * 4 + z_hi * 2 + core


def pairs_from(source_of):
    return [(source_of(index), index) for index in range(512)]


def back_source(table, index):
    x, y, z, core = place(index)
    steps = table[y % 2][core]
    source_x = x if z % 8 >= steps else x - 1
    up = steps < 4 or (steps == 4 and z % 2 == 0)
    return device(source_x, y, z - steps if up else z + 8 - steps, core)


def other_core(index):
    x, y, z, core = place(index)
    return device(x, y, z, 1 - core)


def other_y(index):
    x, y, z, core = place(index)
    return device(x, y ^ 1, z, core)


def inverse(pairs):
    return [(target, source) for source, target in pairs]


def moved(value, pairs):
    return lax.ppermute(value, ("blk", "head"), pairs)


def steps_here(table):
    head = lax.axis_index("head")
    odd = lax.rem(lax.div(head, 4), 2) == 1
    core = lax.rem(head, 2) == 1
    return jnp.where(
        odd,
        jnp.where(core, table[1][1], table[1][0]),
        jnp.where(core, table[0][1], table[0][0]),
    )


def nt(a, b):
    return lax.dot_general(a, b, (((1,), (1,)), ((), ())), preferred_element_type=F32)


def nn(a, b):
    return lax.dot_general(a, b, (((1,), (0,)), ((), ())), preferred_element_type=F32)


def transposed(block):
    return block.astype(F32).T.astype(BF16)


def prep_kernel(
    q_in,
    k_in,
    v_in,
    o_in,
    do_in,
    lse_in,
    ent_in,
    seg_in,
    weight_index_in,
    weights_in,
    msg,
    kv,
    aux,
    q,
    k,
    v,
    o,
    do,
    lse,
    ent,
    seg,
    weight_index,
    weights,
    rows,
    sems,
):
    arriving = [
        pltpu.make_async_copy(source, target, sems.at[n])
        for n, (source, target) in enumerate(
            (
                (weight_index_in, weight_index),
                (weights_in, weights),
                (seg_in, seg),
                (lse_in, lse),
                (ent_in, ent),
                (do_in, do),
                (o_in, o),
                (q_in, q),
                (k_in, k),
                (v_in, v),
            )
        )
    ]
    for copy in arriving:
        copy.start()
    for copy in arriving:
        copy.wait()
    blk = lax.axis_index("blk")
    head = lax.axis_index("head")
    column = pl.multiple_of(lax.div(head, 8) * HD, HD)
    kv[:, :HD] = k[:, pl.ds(column, HD)]
    kv[:, HD:] = v[:, pl.ds(column, HD)]
    docs = weight_index.shape[0]
    tokens = seg[...]
    first = seg[pl.ds(2 * blk, 1), :]
    second = seg[pl.ds(2 * blk + 1, 1), :]
    seg_rows = jnp.concatenate([first, second], axis=1)
    rate = jnp.zeros((1, ROWS), F32)
    for d in range(docs):
        rows[d : d + 1, :HD] = jnp.sum(
            jnp.where(tokens < d, 1.0, 0.0), axis=0, keepdims=True
        )
        rate = jnp.where(seg_rows == d, weights[weight_index[d]], rate)
    starts = jnp.sum(rows[:docs, :HD], axis=1, keepdims=True)
    doc = lax.broadcasted_iota(jnp.int32, (docs, ROWS), 0)
    start = jnp.sum(jnp.where(doc == seg_rows, starts, 0.0), axis=0, keepdims=True)
    aux[...] = jnp.zeros_like(aux)
    aux[0:1, :] = start
    aux[1:2, :] = rate
    rows[...] = jnp.zeros_like(rows)
    for h in range(2):
        columns = slice(h * HD, (h + 1) * HD)
        do_h = do[:, columns]
        msg[h * ROWS : (h + 1) * ROWS, :] = q[:, columns]
        msg[(2 + h) * ROWS : (3 + h) * ROWS, :] = do_h
        product = do_h.astype(F32) * o[:, columns].astype(F32)
        delta = jnp.sum(product.T, axis=0, keepdims=True)
        lse_h = lse[h : h + 1, :]
        const = delta + rate * (ent[h : h + 1, :] - lse_h)
        for at, value in ((0, lse_h), (3, const)):
            for part in range(3):
                piece = value.astype(BF16).astype(F32)
                rows[at + part : at + part + 1, :] = piece
                value = value - piece
        at = 1024 + 32 * h
        msg[at : at + 16, :] = rows[:, :HD].astype(BF16)
        msg[at + 16 : at + 32, :] = rows[:, HD:].astype(BF16)


def prep(*arrays):
    vmem = pl.BlockSpec(memory_space=pltpu.VMEM)
    held = [pltpu.VMEM(array.shape, array.dtype) for array in arrays[:8]]
    held += [pltpu.SMEM(array.shape, array.dtype) for array in arrays[8:]]
    return pl.pallas_call(
        prep_kernel,
        out_shape=(
            jax.ShapeDtypeStruct((MSG, HD), BF16),
            jax.ShapeDtypeStruct((ROWS, 2 * HD), BF16),
            jax.ShapeDtypeStruct((8, ROWS), F32),
        ),
        in_specs=[pl.BlockSpec(memory_space=pltpu.HBM)] * 10,
        out_specs=(vmem,) * 3,
        scratch_shapes=held
        + [pltpu.VMEM((16, ROWS), F32), pltpu.SemaphoreType.DMA((10,))],
        name="prep",
        compiler_params=pltpu.CompilerParams(vmem_limit_bytes=PREP_VMEM_LIMIT),
    )(*arrays)


def both(row):
    return jnp.concatenate([row, row], axis=1)


def row_terms(msg):
    halves = [msg[at : at + 16, :].astype(F32) for at in range(4 * ROWS, MSG, 16)]

    def whole(row):
        return jnp.concatenate(
            [
                half[row : row + 1, :] + half[row + 1 : row + 2, :] + half[row + 2 : row + 3, :]
                for half in halves
            ],
            axis=1,
        )

    return whole(0) * LOG2E, whole(3)


def probs_and_dscores(key_block, value_block, msg, rate, visible):
    lse2, const = row_terms(msg)
    scores = nt(key_block, msg[: 2 * ROWS, :])
    probs = jnp.where(visible, jnp.exp2(scores * (SCALE * LOG2E) - lse2), 0.0)
    dprobs = nt(value_block, msg[2 * ROWS : 4 * ROWS, :])
    dscores = probs * (dprobs - const - scores * rate)
    return probs.astype(BF16), dscores.astype(BF16)


def sums_of(messages, key_block, value_block, rate, visible, put_query_sum):
    key_turned = transposed(key_block)
    key_sum = value_sum = before = None
    for n, msg in enumerate((*messages, None)):
        here = None
        if msg is not None:
            here = probs_and_dscores(key_block, value_block, msg, rate, visible)
        if before is not None:
            probs, dscores = before
            past = messages[n - 1]
            put_query_sum(n - 1, nn(key_turned, dscores))
            key_add = nn(dscores, past[: 2 * ROWS, :])
            value_add = nn(probs, past[2 * ROWS : 4 * ROWS, :])
            key_sum = key_add if key_sum is None else key_sum + key_add
            value_sum = value_add if value_sum is None else value_sum + value_add
        before = here
    return key_sum, value_sum


def block_place(table, start):
    key_start = ((lax.axis_index("blk") - steps_here(table)) * ROWS).astype(F32)
    return start - key_start, key_start + (ROWS - 1) >= jnp.min(start)


def earlier_sums(table, messages, kv, aux, put):
    reach, _ = block_place(table, aux[0:1, :])
    key_at = lax.broadcasted_iota(jnp.int32, (ROWS, 2 * ROWS), 0).astype(F32)
    return sums_of(
        messages,
        kv[:, :HD],
        kv[:, HD:],
        both(aux[1:2, :] * SCALE),
        key_at >= both(reach),
        put,
    )


def early_kernel(own, y, cross, kv_far, aux, dq_own, far, dq):
    _, seen = block_place(FAR, aux[0:1, :])

    @pl.when(jnp.logical_not(seen))
    def _():
        dq[0] = dq_own[0]
        dq[1:] = jnp.zeros_like(dq[1:])
        far[...] = jnp.zeros_like(far)

    @pl.when(seen)
    def _():
        def put(n, query_sum):
            dq[n] = dq_own[0] + query_sum if n == 0 else query_sum

        key_sum, value_sum = earlier_sums(FAR, (own, y, cross), kv_far, aux, put)
        far[:, :HD] = key_sum
        far[:, HD:] = value_sum


def late_kernel(
    own, core, y, cross, kv_far, kv_near, aux, far_in, dq_in, far, near, dq
):
    _, far_seen = block_place(FAR, aux[0:1, :])
    _, near_seen = block_place(NEAR, aux[0:1, :])

    @pl.when(jnp.logical_not(near_seen))
    def _():
        dq[:3] = dq_in[...]
        dq[3] = jnp.zeros_like(dq[3])
        near[...] = jnp.zeros_like(near)

    @pl.when(near_seen)
    def _():
        def put(n, query_sum):
            dq[n] = dq_in[n] + query_sum if n < 3 else query_sum

        key_sum, value_sum = earlier_sums(NEAR, (own, y, cross, core), kv_near, aux, put)
        near[:, :HD] = key_sum.astype(BF16)
        near[:, HD:] = value_sum.astype(BF16)

    @pl.when(jnp.logical_not(far_seen))
    def _():
        far[...] = far_in[...].astype(BF16)

    @pl.when(far_seen)
    def _():
        def put(n, query_sum):
            dq[3] += query_sum

        key_sum, value_sum = earlier_sums(FAR, (core,), kv_far, aux, put)
        far[:, :HD] = (far_in[:, :HD] + key_sum).astype(BF16)
        far[:, HD:] = (far_in[:, HD:] + value_sum).astype(BF16)


def kernel_call(kernel, name, out_shape, flops, *arrays):
    vmem = pl.BlockSpec(memory_space=pltpu.VMEM)
    return pl.pallas_call(
        kernel,
        out_shape=out_shape,
        in_specs=[vmem] * len(arrays),
        out_specs=(vmem,) * len(out_shape),
        name=name,
        compiler_params=pltpu.CompilerParams(vmem_limit_bytes=VMEM_LIMIT),
        cost_estimate=pl.CostEstimate(flops=flops, bytes_accessed=1 << 20, transcendentals=0),
    )(*arrays)


def own_kernel(msg, kv, aux, dq, dkv):
    blk = lax.axis_index("blk")
    threshold = aux[0:1, :] - (blk * ROWS).astype(F32)
    key_at = lax.broadcasted_iota(jnp.int32, (ROWS, ROWS), 0)
    query_at = lax.broadcasted_iota(jnp.int32, (ROWS, ROWS), 1)
    causal = both(jnp.where(key_at <= query_at, key_at, -1).astype(F32))

    def put(n, query_sum):
        dq[n] = query_sum

    key_sum, value_sum = sums_of(
        (msg,),
        kv[:, :HD],
        kv[:, HD:],
        both(aux[1:2, :] * SCALE),
        causal >= both(jnp.maximum(threshold, 0.0)),
        put,
    )
    dkv[:, :HD] = key_sum
    dkv[:, HD:] = value_sum


def turn_kernel(dq, send, keep):
    for n, (kept, sent) in enumerate(((0, 3), (1, 2))):
        at = slice(2 * n * ROWS, 2 * (n + 1) * ROWS)
        keep[at, :] = dq[kept].T
        send[at, :] = dq[sent].T.astype(BF16)


def query_kernel(dq_keep, dq_core, dq_y, grad_query):
    for h in range(2):
        at = slice(h * ROWS, (h + 1) * ROWS)
        total = dq_keep[at, :] + dq_core[at, :].astype(F32) + dq_y[at, :].astype(F32)
        grad_query[:, h * HD : (h + 1) * HD] = (total * SCALE).astype(BF16)


def terms_kernel(own, far, near, terms):
    share = terms.shape[1]
    for n, head in enumerate(HEAD_ORDER):
        at = slice(head * share, (head + 1) * share)
        total = own[at, :] + far[at, :].astype(F32) + near[at, :].astype(F32)
        terms[n] = total.astype(BF16)


def key_value_kernel(terms, grad_key, grad_value):
    for g in range(2):
        total = 0.0
        for n, head in enumerate(HEAD_ORDER):
            if head // 8 == g:
                total = total + terms[n].astype(F32)
        grad_key[:, g * HD : (g + 1) * HD] = (total[:, :HD] * SCALE).astype(BF16)
        grad_value[:, g * HD : (g + 1) * HD] = total[:, HD:].astype(BF16)


def local(
    query,
    key,
    value,
    output,
    grad_output,
    log_norm,
    entropy,
    segment_ids,
    weight_index,
    penalty_weights,
):
    to_core = pairs_from(other_core)
    to_y = pairs_from(other_y)
    to_cross = pairs_from(lambda index: other_y(other_core(index)))
    back_near = pairs_from(functools.partial(back_source, NEAR))
    back_far = pairs_from(functools.partial(back_source, FAR))
    msg, kv, aux = prep(
        query,
        key,
        value,
        output,
        grad_output,
        log_norm,
        entropy,
        segment_ids.reshape(-1, HD),
        weight_index,
        penalty_weights,
    )
    msg_core = moved(msg, to_core)
    kv_near = moved(kv, back_near)
    msg_y = moved(msg, to_y)
    kv_far = moved(kv, back_far)
    msg_cross = moved(msg, to_cross)
    sums = functools.partial(jax.ShapeDtypeStruct, dtype=F32)
    pair = jax.ShapeDtypeStruct((ROWS, 2 * HD), BF16)
    dq_own, dkv_own = kernel_call(
        own_kernel,
        "own",
        (sums((1, HD, 2 * ROWS)), sums((ROWS, 2 * HD))),
        OWN_FLOPS,
        msg,
        kv,
        aux,
    )
    dkv_far, dq = kernel_call(
        early_kernel,
        "early",
        (sums((ROWS, 2 * HD)), sums((3, HD, 2 * ROWS))),
        EARLY_FLOPS,
        msg,
        msg_y,
        msg_cross,
        kv_far,
        aux,
        dq_own,
    )
    dkv_far, dkv_near, dq = kernel_call(
        late_kernel,
        "late",
        (pair, pair, sums((4, HD, 2 * ROWS))),
        LATE_FLOPS,
        msg,
        msg_core,
        msg_y,
        msg_cross,
        kv_far,
        kv_near,
        aux,
        dkv_far,
        dq,
    )
    got_near = moved(dkv_near, inverse(back_near))
    got_far = moved(dkv_far, inverse(back_far))
    dq_send, dq_keep = kernel_call(
        turn_kernel,
        "turn",
        (jax.ShapeDtypeStruct((4 * ROWS, HD), BF16), sums((4 * ROWS, HD))),
        TURN_FLOPS,
        dq,
    )
    dq_core = moved(dq_send, to_core)
    dq_pass = (dq_keep[512:] + dq_core[512:].astype(F32)).astype(BF16)
    share = jax.ShapeDtypeStruct((16, ROWS // 16, 2 * HD), BF16)
    (terms,) = kernel_call(terms_kernel, "terms", (share,), 0, dkv_own, got_far, got_near)
    dq_y = moved(dq_pass, to_y)
    terms = lax.all_to_all(terms, "head", 0, 0, axis_index_groups=[HEAD_ORDER])
    (grad_query,) = kernel_call(query_kernel, "query", (pair,), QUERY_FLOPS, dq_keep, dq_core, dq_y)
    result = jax.ShapeDtypeStruct((terms.shape[1], 2 * HD), BF16)
    return (grad_query, *kernel_call(key_value_kernel, "key_value", (result, result), 0, terms))


def solution(mesh):
    in_specs = (
        P("blk", "head"),
        P("blk", None),
        P("blk", None),
        P("blk", "head"),
        P("blk", "head"),
        P("head", "blk"),
        P("head", "blk"),
        P(),
        P(),
        P(),
    )
    out_specs = (P("blk", "head"), P(("blk", "head"), None), P(("blk", "head"), None))
    return jax.shard_map(local, mesh=mesh, in_specs=in_specs, out_specs=out_specs, check_vma=False)
```

```python
import functools
import math

import jax
import jax.numpy as jnp
from jax import lax
from jax.experimental import pallas as pl
from jax.experimental.pallas import tpu as pltpu
from jax.sharding import PartitionSpec as P

HD = 128
ROWS = 256
SCALE = HD ** (-0.5)
LOG2E = math.log2(math.e)
MSG = 4 * ROWS + 64
GROUP = 8
F32 = jnp.float32
OWN_FLOPS = 1 << 28
EARLY_FLOPS = 1 << 34
LATE_FLOPS = 1 << 30
TURN_FLOPS = 1 << 27
QUERY_FLOPS = 1 << 34
BF16 = jnp.bfloat16
VMEM_LIMIT = 24 * 1024 * 1024

NEAR = ((1, 7), (2, 6))
FAR = ((3, 5), (4, 8))

HEAD_ORDER = [y * 4 + z_hi * 2 + core for z_hi in (1, 0) for y in range(4) for core in range(2)]


def place(index):
    blk, head = divmod(index, 16)
    x, z_lo = divmod(blk, 8)
    y, rest = divmod(head, 4)
    z_hi, core = divmod(rest, 2)
    return x, y, z_hi * 8 + z_lo, core


def device(x, y, z, core):
    z_hi, z_lo = divmod(z % 16, 8)
    return ((x % 4) * 8 + z_lo) * 16 + (y % 4) * 4 + z_hi * 2 + core


def pairs_from(source_of):
    return [(source_of(index), index) for index in range(512)]


def back_source(table, index):
    x, y, z, core = place(index)
    steps = table[y % 2][core]
    source_x = x if z % 8 >= steps else x - 1
    up = steps < 4 or (steps == 4 and z % 2 == 0)
    return device(source_x, y, z - steps if up else z + 8 - steps, core)


def other_core(index):
    x, y, z, core = place(index)
    return device(x, y, z, 1 - core)


def other_y(index):
    x, y, z, core = place(index)
    return device(x, y ^ 1, z, core)


def inverse(pairs):
    return [(target, source) for source, target in pairs]


def moved(value, pairs):
    return lax.ppermute(value, ("blk", "head"), pairs)


def steps_here(table):
    head = lax.axis_index("head")
    odd = lax.rem(lax.div(head, 4), 2) == 1
    core = lax.rem(head, 2) == 1
    return jnp.where(
        odd,
        jnp.where(core, table[1][1], table[1][0]),
        jnp.where(core, table[0][1], table[0][0]),
    )


def nt(a, b):
    return lax.dot_general(a, b, (((1,), (1,)), ((), ())), preferred_element_type=F32)


def nn(a, b):
    return lax.dot_general(a, b, (((1,), (0,)), ((), ())), preferred_element_type=F32)


def transposed(block):
    return block.astype(F32).T.astype(BF16)


def prep_kernel(
    q_in,
    k_in,
    v_in,
    o_in,
    do_in,
    lse_in,
    ent_in,
    seg_in,
    weight_index_in,
    weights_in,
    msg,
    kv,
    aux,
    q,
    k,
    v,
    o,
    do,
    lse,
    ent,
    seg,
    weight_index,
    weights,
    rows,
    sems,
):
    arriving = [
        pltpu.make_async_copy(source, target, sems.at[n])
        for n, (source, target) in enumerate(
            (
                (weight_index_in, weight_index),
                (weights_in, weights),
                (seg_in, seg),
                (lse_in, lse),
                (ent_in, ent),
                (do_in, do),
                (o_in, o),
                (q_in, q),
                (k_in, k),
                (v_in, v),
            )
        )
    ]
    for copy in arriving:
        copy.start()
    for copy in arriving:
        copy.wait()
    blk = lax.axis_index("blk")
    head = lax.axis_index("head")
    column = pl.multiple_of(lax.div(head, 8) * HD, HD)
    kv[:, :HD] = k[:, pl.ds(column, HD)]
    kv[:, HD:] = v[:, pl.ds(column, HD)]
    docs = weight_index.shape[0]
    tokens = seg[...]
    first = seg[pl.ds(2 * blk, 1), :]
    second = seg[pl.ds(2 * blk + 1, 1), :]
    seg_rows = jnp.concatenate([first, second], axis=1)
    rate = jnp.zeros((1, ROWS), F32)
    for d in range(docs):
        rows[d : d + 1, :HD] = jnp.sum(
            jnp.where(tokens < d, 1.0, 0.0), axis=0, keepdims=True
        )
        rate = jnp.where(seg_rows == d, weights[weight_index[d]], rate)
    starts = jnp.sum(rows[:docs, :HD], axis=1, keepdims=True)
    doc = lax.broadcasted_iota(jnp.int32, (docs, ROWS), 0)
    start = jnp.sum(jnp.where(doc == seg_rows, starts, 0.0), axis=0, keepdims=True)
    aux[...] = jnp.zeros_like(aux)
    aux[0:1, :] = start
    aux[1:2, :] = rate
    rows[...] = jnp.zeros_like(rows)
    for h in range(2):
        columns = slice(h * HD, (h + 1) * HD)
        do_h = do[:, columns]
        msg[h * ROWS : (h + 1) * ROWS, :] = q[:, columns]
        msg[(2 + h) * ROWS : (3 + h) * ROWS, :] = do_h
        product = do_h.astype(F32) * o[:, columns].astype(F32)
        delta = jnp.sum(product.T, axis=0, keepdims=True)
        lse_h = lse[h : h + 1, :]
        const = delta + rate * (ent[h : h + 1, :] - lse_h)
        for at, value in ((0, lse_h), (3, const)):
            for part in range(3):
                piece = value.astype(BF16).astype(F32)
                rows[at + part : at + part + 1, :] = piece
                value = value - piece
        at = 1024 + 32 * h
        msg[at : at + 16, :] = rows[:, :HD].astype(BF16)
        msg[at + 16 : at + 32, :] = rows[:, HD:].astype(BF16)


def prep(*arrays):
    vmem = pl.BlockSpec(memory_space=pltpu.VMEM)
    held = [pltpu.VMEM(array.shape, array.dtype) for array in arrays[:8]]
    held += [pltpu.SMEM(array.shape, array.dtype) for array in arrays[8:]]
    return pl.pallas_call(
        prep_kernel,
        out_shape=(
            jax.ShapeDtypeStruct((MSG, HD), BF16),
            jax.ShapeDtypeStruct((ROWS, 2 * HD), BF16),
            jax.ShapeDtypeStruct((8, ROWS), F32),
        ),
        in_specs=[pl.BlockSpec(memory_space=pltpu.HBM)] * 10,
        out_specs=(vmem,) * 3,
        scratch_shapes=held
        + [pltpu.VMEM((16, ROWS), F32), pltpu.SemaphoreType.DMA((10,))],
        name="prep",
        compiler_params=pltpu.CompilerParams(vmem_limit_bytes=VMEM_LIMIT),
    )(*[pltpu.with_memory_space_constraint(array, pltpu.HBM) for array in arrays])


def both(row):
    return jnp.concatenate([row, row], axis=1)


def row_terms(msg):
    halves = [msg[at : at + 16, :].astype(F32) for at in range(4 * ROWS, MSG, 16)]

    def whole(row):
        return jnp.concatenate(
            [
                half[row : row + 1, :] + half[row + 1 : row + 2, :] + half[row + 2 : row + 3, :]
                for half in halves
            ],
            axis=1,
        )

    return whole(0) * LOG2E, whole(3)


def probs_and_dscores(key_block, value_block, msg, rate, visible):
    lse2, const = row_terms(msg)
    scores = nt(key_block, msg[: 2 * ROWS, :])
    probs = jnp.where(visible, jnp.exp2(scores * (SCALE * LOG2E) - lse2), 0.0)
    dprobs = nt(value_block, msg[2 * ROWS : 4 * ROWS, :])
    dscores = probs * (dprobs - const - scores * rate)
    return probs.astype(BF16), dscores.astype(BF16)


def sums_of(messages, key_block, value_block, rate, visible, put_query_sum):
    key_turned = transposed(key_block)
    key_sum = value_sum = before = None
    for n, msg in enumerate((*messages, None)):
        here = None
        if msg is not None:
            here = probs_and_dscores(key_block, value_block, msg, rate, visible)
        if before is not None:
            probs, dscores = before
            past = messages[n - 1]
            put_query_sum(n - 1, nn(key_turned, dscores))
            key_add = nn(dscores, past[: 2 * ROWS, :])
            value_add = nn(probs, past[2 * ROWS : 4 * ROWS, :])
            key_sum = key_add if key_sum is None else key_sum + key_add
            value_sum = value_add if value_sum is None else value_sum + value_add
        before = here
    return key_sum, value_sum


def block_place(table, start):
    key_start = ((lax.axis_index("blk") - steps_here(table)) * ROWS).astype(F32)
    return start - key_start, key_start + (ROWS - 1) >= jnp.min(start)


def earlier_sums(table, messages, kv, aux, put):
    reach, _ = block_place(table, aux[0:1, :])
    key_at = lax.broadcasted_iota(jnp.int32, (ROWS, 2 * ROWS), 0).astype(F32)
    return sums_of(
        messages,
        kv[:, :HD],
        kv[:, HD:],
        both(aux[1:2, :] * SCALE),
        key_at >= both(reach),
        put,
    )


def early_kernel(own, y, cross, kv_far, aux, dq_own, far, dq):
    _, seen = block_place(FAR, aux[0:1, :])

    @pl.when(jnp.logical_not(seen))
    def _():
        dq[0] = dq_own[0]
        dq[1:] = jnp.zeros_like(dq[1:])
        far[...] = jnp.zeros_like(far)

    @pl.when(seen)
    def _():
        def put(n, query_sum):
            dq[n] = dq_own[0] + query_sum if n == 0 else query_sum

        key_sum, value_sum = earlier_sums(FAR, (own, y, cross), kv_far, aux, put)
        far[:, :HD] = key_sum
        far[:, HD:] = value_sum


def late_kernel(
    own, core, y, cross, kv_far, kv_near, aux, far_in, dq_in, far, near, dq
):
    _, far_seen = block_place(FAR, aux[0:1, :])
    _, near_seen = block_place(NEAR, aux[0:1, :])

    @pl.when(jnp.logical_not(near_seen))
    def _():
        dq[:3] = dq_in[...]
        dq[3] = jnp.zeros_like(dq[3])
        near[...] = jnp.zeros_like(near)

    @pl.when(near_seen)
    def _():
        def put(n, query_sum):
            dq[n] = dq_in[n] + query_sum if n < 3 else query_sum

        key_sum, value_sum = earlier_sums(NEAR, (own, y, cross, core), kv_near, aux, put)
        near[:, :HD] = key_sum.astype(BF16)
        near[:, HD:] = value_sum.astype(BF16)

    @pl.when(jnp.logical_not(far_seen))
    def _():
        far[...] = far_in[...].astype(BF16)

    @pl.when(far_seen)
    def _():
        def put(n, query_sum):
            dq[3] += query_sum

        key_sum, value_sum = earlier_sums(FAR, (core,), kv_far, aux, put)
        far[:, :HD] = (far_in[:, :HD] + key_sum).astype(BF16)
        far[:, HD:] = (far_in[:, HD:] + value_sum).astype(BF16)


def kernel_call(kernel, name, out_shape, flops, *arrays):
    vmem = pl.BlockSpec(memory_space=pltpu.VMEM)
    return pl.pallas_call(
        kernel,
        out_shape=out_shape,
        in_specs=[vmem] * len(arrays),
        out_specs=(vmem,) * len(out_shape),
        name=name,
        compiler_params=pltpu.CompilerParams(vmem_limit_bytes=VMEM_LIMIT),
        cost_estimate=pl.CostEstimate(flops=flops, bytes_accessed=1 << 20, transcendentals=0),
    )(*arrays)


def own_kernel(msg, kv, aux, dq, dkv):
    blk = lax.axis_index("blk")
    threshold = aux[0:1, :] - (blk * ROWS).astype(F32)
    key_at = lax.broadcasted_iota(jnp.int32, (ROWS, ROWS), 0)
    query_at = lax.broadcasted_iota(jnp.int32, (ROWS, ROWS), 1)
    causal = both(jnp.where(key_at <= query_at, key_at, -1).astype(F32))

    def put(n, query_sum):
        dq[n] = query_sum

    key_sum, value_sum = sums_of(
        (msg,),
        kv[:, :HD],
        kv[:, HD:],
        both(aux[1:2, :] * SCALE),
        causal >= both(jnp.maximum(threshold, 0.0)),
        put,
    )
    dkv[:, :HD] = key_sum
    dkv[:, HD:] = value_sum


def turn_kernel(dq, send, keep):
    for n, (kept, sent) in enumerate(((0, 3), (1, 2))):
        at = slice(2 * n * ROWS, 2 * (n + 1) * ROWS)
        keep[at, :] = dq[kept].T
        send[at, :] = dq[sent].T.astype(BF16)


def query_kernel(dq_keep, dq_core, dq_y, grad_query):
    for h in range(2):
        at = slice(h * ROWS, (h + 1) * ROWS)
        total = dq_keep[at, :] + dq_core[at, :].astype(F32) + dq_y[at, :].astype(F32)
        grad_query[:, h * HD : (h + 1) * HD] = (total * SCALE).astype(BF16)


def terms_kernel(own, far, near, terms):
    share = terms.shape[1]
    for n, head in enumerate(HEAD_ORDER):
        at = slice(head * share, (head + 1) * share)
        total = own[at, :] + far[at, :].astype(F32) + near[at, :].astype(F32)
        terms[n] = total.astype(BF16)


def key_value_kernel(terms, grad_key, grad_value):
    for g in range(2):
        total = 0.0
        for n, head in enumerate(HEAD_ORDER):
            if head // 8 == g:
                total = total + terms[n].astype(F32)
        grad_key[:, g * HD : (g + 1) * HD] = (total[:, :HD] * SCALE).astype(BF16)
        grad_value[:, g * HD : (g + 1) * HD] = total[:, HD:].astype(BF16)


def local(
    query,
    key,
    value,
    output,
    grad_output,
    log_norm,
    entropy,
    segment_ids,
    weight_index,
    penalty_weights,
):
    to_core = pairs_from(other_core)
    to_y = pairs_from(other_y)
    to_cross = pairs_from(lambda index: other_y(other_core(index)))
    back_near = pairs_from(functools.partial(back_source, NEAR))
    back_far = pairs_from(functools.partial(back_source, FAR))
    msg, kv, aux = prep(
        query,
        key,
        value,
        output,
        grad_output,
        log_norm,
        entropy,
        segment_ids.reshape(-1, HD),
        weight_index,
        penalty_weights,
    )
    msg_core = moved(msg, to_core)
    kv_near = moved(kv, back_near)
    msg_y = moved(msg, to_y)
    kv_far = moved(kv, back_far)
    msg_cross = moved(msg, to_cross)
    sums = functools.partial(jax.ShapeDtypeStruct, dtype=F32)
    pair = jax.ShapeDtypeStruct((ROWS, 2 * HD), BF16)
    dq_own, dkv_own = kernel_call(
        own_kernel,
        "own",
        (sums((1, HD, 2 * ROWS)), sums((ROWS, 2 * HD))),
        OWN_FLOPS,
        msg,
        kv,
        aux,
    )
    dkv_far, dq = kernel_call(
        early_kernel,
        "early",
        (sums((ROWS, 2 * HD)), sums((3, HD, 2 * ROWS))),
        EARLY_FLOPS,
        msg,
        msg_y,
        msg_cross,
        kv_far,
        aux,
        dq_own,
    )
    dkv_far, dkv_near, dq = kernel_call(
        late_kernel,
        "late",
        (pair, pair, sums((4, HD, 2 * ROWS))),
        LATE_FLOPS,
        msg,
        msg_core,
        msg_y,
        msg_cross,
        kv_far,
        kv_near,
        aux,
        dkv_far,
        dq,
    )
    got_near = moved(dkv_near, inverse(back_near))
    got_far = moved(dkv_far, inverse(back_far))
    dq_send, dq_keep = kernel_call(
        turn_kernel,
        "turn",
        (jax.ShapeDtypeStruct((4 * ROWS, HD), BF16), sums((4 * ROWS, HD))),
        TURN_FLOPS,
        dq,
    )
    dq_core = moved(dq_send, to_core)
    dq_pass = (dq_keep[512:] + dq_core[512:].astype(F32)).astype(BF16)
    share = jax.ShapeDtypeStruct((16, ROWS // 16, 2 * HD), BF16)
    (terms,) = kernel_call(terms_kernel, "terms", (share,), 0, dkv_own, got_far, got_near)
    dq_y = moved(dq_pass, to_y)
    terms = lax.all_to_all(terms, "head", 0, 0, axis_index_groups=[HEAD_ORDER])
    (grad_query,) = kernel_call(query_kernel, "query", (pair,), QUERY_FLOPS, dq_keep, dq_core, dq_y)
    result = jax.ShapeDtypeStruct((terms.shape[1], 2 * HD), BF16)
    return (grad_query, *kernel_call(key_value_kernel, "key_value", (result, result), 0, terms))


def solution(mesh):
    in_specs = (
        P("blk", "head"),
        P("blk", None),
        P("blk", None),
        P("blk", "head"),
        P("blk", "head"),
        P("head", "blk"),
        P("head", "blk"),
        P(),
        P(),
        P(),
    )
    out_specs = (P("blk", "head"), P(("blk", "head"), None), P(("blk", "head"), None))
    return jax.shard_map(local, mesh=mesh, in_specs=in_specs, out_specs=out_specs, check_vma=False)
```

```python
import functools
import math

import jax
import jax.numpy as jnp
from jax import lax
from jax.experimental import pallas as pl
from jax.experimental.pallas import tpu as pltpu
from jax.sharding import PartitionSpec as P

HD = 128
ROWS = 256
SCALE = HD ** (-0.5)
LOG2E = math.log2(math.e)
MSG = 4 * ROWS + 64
GROUP = 8
F32 = jnp.float32
OWN_FLOPS = 1 << 28
EARLY_FLOPS = 1 << 34
LATE_FLOPS = 1 << 30
TURN_FLOPS = 1 << 27
QUERY_FLOPS = 1 << 34
BF16 = jnp.bfloat16
VMEM_LIMIT = 24 * 1024 * 1024

NEAR = ((1, 7), (2, 6))
FAR = ((3, 5), (4, 8))

HEAD_ORDER = [y * 4 + z_hi * 2 + core for z_hi in (1, 0) for y in range(4) for core in range(2)]


def place(index):
    blk, head = divmod(index, 16)
    x, z_lo = divmod(blk, 8)
    y, rest = divmod(head, 4)
    z_hi, core = divmod(rest, 2)
    return x, y, z_hi * 8 + z_lo, core


def device(x, y, z, core):
    z_hi, z_lo = divmod(z % 16, 8)
    return ((x % 4) * 8 + z_lo) * 16 + (y % 4) * 4 + z_hi * 2 + core


def pairs_from(source_of):
    return [(source_of(index), index) for index in range(512)]


def back_source(table, index):
    x, y, z, core = place(index)
    steps = table[y % 2][core]
    source_x = x if z % 8 >= steps else x - 1
    up = steps < 4 or (steps == 4 and z % 2 == 0)
    return device(source_x, y, z - steps if up else z + 8 - steps, core)


def other_core(index):
    x, y, z, core = place(index)
    return device(x, y, z, 1 - core)


def other_y(index):
    x, y, z, core = place(index)
    return device(x, y ^ 1, z, core)


def inverse(pairs):
    return [(target, source) for source, target in pairs]


def moved(value, pairs):
    return lax.ppermute(value, ("blk", "head"), pairs)


def steps_here(table):
    head = lax.axis_index("head")
    odd = lax.rem(lax.div(head, 4), 2) == 1
    core = lax.rem(head, 2) == 1
    return jnp.where(
        odd,
        jnp.where(core, table[1][1], table[1][0]),
        jnp.where(core, table[0][1], table[0][0]),
    )


def nt(a, b):
    return lax.dot_general(a, b, (((1,), (1,)), ((), ())), preferred_element_type=F32)


def nn(a, b):
    return lax.dot_general(a, b, (((1,), (0,)), ((), ())), preferred_element_type=F32)


def transposed(block):
    return block.astype(F32).T.astype(BF16)


def prep_kernel(
    q_in,
    k_in,
    v_in,
    o_in,
    do_in,
    lse_in,
    ent_in,
    seg_in,
    weight_index_in,
    weights_in,
    msg,
    kv,
    aux,
    q,
    k,
    v,
    o,
    do,
    lse,
    ent,
    seg,
    weight_index,
    weights,
    rows,
    sems,
):
    arriving = [
        pltpu.make_async_copy(source, target, sems.at[n])
        for n, (source, target) in enumerate(
            (
                (weight_index_in, weight_index),
                (weights_in, weights),
                (seg_in, seg),
                (lse_in, lse),
                (ent_in, ent),
                (do_in, do),
                (o_in, o),
                (q_in, q),
                (k_in, k),
                (v_in, v),
            )
        )
    ]
    for copy in arriving:
        copy.start()
    for copy in arriving:
        copy.wait()
    blk = lax.axis_index("blk")
    head = lax.axis_index("head")
    column = pl.multiple_of(lax.div(head, 8) * HD, HD)
    kv[:, :HD] = k[:, pl.ds(column, HD)]
    kv[:, HD:] = v[:, pl.ds(column, HD)]
    docs = weight_index.shape[0]
    tokens = seg[...]
    first = seg[pl.ds(2 * blk, 1), :]
    second = seg[pl.ds(2 * blk + 1, 1), :]
    seg_rows = jnp.concatenate([first, second], axis=1)
    rate = jnp.zeros((1, ROWS), F32)
    for d in range(docs):
        rows[d : d + 1, :HD] = jnp.sum(
            jnp.where(tokens < d, 1.0, 0.0), axis=0, keepdims=True
        )
        rate = jnp.where(seg_rows == d, weights[weight_index[d]], rate)
    starts = jnp.sum(rows[:docs, :HD], axis=1, keepdims=True)
    doc = lax.broadcasted_iota(jnp.int32, (docs, ROWS), 0)
    start = jnp.sum(jnp.where(doc == seg_rows, starts, 0.0), axis=0, keepdims=True)
    aux[...] = jnp.zeros_like(aux)
    aux[0:1, :] = start
    aux[1:2, :] = rate
    rows[...] = jnp.zeros_like(rows)
    for h in range(2):
        columns = slice(h * HD, (h + 1) * HD)
        do_h = do[:, columns]
        msg[h * ROWS : (h + 1) * ROWS, :] = q[:, columns]
        msg[(2 + h) * ROWS : (3 + h) * ROWS, :] = do_h
        product = do_h.astype(F32) * o[:, columns].astype(F32)
        delta = jnp.sum(product.T, axis=0, keepdims=True)
        lse_h = lse[h : h + 1, :]
        const = delta + rate * (ent[h : h + 1, :] - lse_h)
        for at, value in ((0, lse_h), (3, const)):
            for part in range(3):
                piece = value.astype(BF16).astype(F32)
                rows[at + part : at + part + 1, :] = piece
                value = value - piece
        at = 1024 + 32 * h
        msg[at : at + 16, :] = rows[:, :HD].astype(BF16)
        msg[at + 16 : at + 32, :] = rows[:, HD:].astype(BF16)


def prep(*arrays):
    vmem = pl.BlockSpec(memory_space=pltpu.VMEM)
    held = [pltpu.VMEM(array.shape, array.dtype) for array in arrays[:8]]
    held += [pltpu.SMEM(array.shape, array.dtype) for array in arrays[8:]]
    return pl.pallas_call(
        prep_kernel,
        out_shape=(
            jax.ShapeDtypeStruct((MSG, HD), BF16),
            jax.ShapeDtypeStruct((ROWS, 2 * HD), BF16),
            jax.ShapeDtypeStruct((8, ROWS), F32),
        ),
        in_specs=[pl.BlockSpec(memory_space=pltpu.HBM)] * 10,
        out_specs=(vmem,) * 3,
        scratch_shapes=held
        + [pltpu.VMEM((16, ROWS), F32), pltpu.SemaphoreType.DMA((10,))],
        name="prep",
        compiler_params=pltpu.CompilerParams(vmem_limit_bytes=VMEM_LIMIT),
    )(*[pltpu.with_memory_space_constraint(array, pltpu.HBM) for array in arrays])


def both(row):
    return jnp.concatenate([row, row], axis=1)


def row_terms(msg):
    halves = [msg[at : at + 16, :].astype(F32) for at in range(4 * ROWS, MSG, 16)]

    def whole(row):
        return jnp.concatenate(
            [
                half[row : row + 1, :] + half[row + 1 : row + 2, :] + half[row + 2 : row + 3, :]
                for half in halves
            ],
            axis=1,
        )

    return whole(0) * LOG2E, whole(3)


def probs_and_dscores(key_block, value_block, msg, rate, visible):
    lse2, const = row_terms(msg)
    scores = nt(key_block, msg[: 2 * ROWS, :])
    probs = jnp.where(visible, jnp.exp2(scores * (SCALE * LOG2E) - lse2), 0.0)
    dprobs = nt(value_block, msg[2 * ROWS : 4 * ROWS, :])
    dscores = probs * (dprobs - const - scores * rate)
    return probs.astype(BF16), dscores.astype(BF16)


def sums_of(messages, key_block, value_block, rate, visible, put_query_sum):
    key_turned = transposed(key_block)
    key_sum = value_sum = before = None
    for n, msg in enumerate((*messages, None)):
        here = None
        if msg is not None:
            here = probs_and_dscores(key_block, value_block, msg, rate, visible)
        if before is not None:
            probs, dscores = before
            past = messages[n - 1]
            put_query_sum(n - 1, nn(key_turned, dscores))
            key_add = nn(dscores, past[: 2 * ROWS, :])
            value_add = nn(probs, past[2 * ROWS : 4 * ROWS, :])
            key_sum = key_add if key_sum is None else key_sum + key_add
            value_sum = value_add if value_sum is None else value_sum + value_add
        before = here
    return key_sum, value_sum


def block_place(table, start):
    key_start = ((lax.axis_index("blk") - steps_here(table)) * ROWS).astype(F32)
    return start - key_start, key_start + (ROWS - 1) >= jnp.min(start)


def earlier_sums(table, messages, kv, aux, put):
    reach, _ = block_place(table, aux[0:1, :])
    key_at = lax.broadcasted_iota(jnp.int32, (ROWS, 2 * ROWS), 0).astype(F32)
    return sums_of(
        messages,
        kv[:, :HD],
        kv[:, HD:],
        both(aux[1:2, :] * SCALE),
        key_at >= both(reach),
        put,
    )


def early_kernel(own, y, kv_far, aux, dq_own, far, dq):
    _, seen = block_place(FAR, aux[0:1, :])

    @pl.when(jnp.logical_not(seen))
    def _():
        dq[0] = dq_own[0]
        dq[1:] = jnp.zeros_like(dq[1:])
        far[...] = jnp.zeros_like(far)

    @pl.when(seen)
    def _():
        def put(n, query_sum):
            dq[n] = dq_own[0] + query_sum if n == 0 else query_sum

        key_sum, value_sum = earlier_sums(FAR, (own, y), kv_far, aux, put)
        far[:, :HD] = key_sum
        far[:, HD:] = value_sum


def late_kernel(own, y, kv_near, kv_far, other, aux, far_in, dq_in, far, near, dq):
    core, cross = other.at[:MSG, :], other.at[MSG:, :]
    _, far_seen = block_place(FAR, aux[0:1, :])
    _, near_seen = block_place(NEAR, aux[0:1, :])

    @pl.when(jnp.logical_not(near_seen))
    def _():
        dq[:2] = dq_in[...]
        dq[2:] = jnp.zeros_like(dq[2:])
        near[...] = jnp.zeros_like(near)

    @pl.when(near_seen)
    def _():
        def put(n, query_sum):
            dq[n] = dq_in[n] + query_sum if n < 2 else query_sum

        key_sum, value_sum = earlier_sums(NEAR, (own, y, core, cross), kv_near, aux, put)
        near[:, :HD] = key_sum.astype(BF16)
        near[:, HD:] = value_sum.astype(BF16)

    @pl.when(jnp.logical_not(far_seen))
    def _():
        far[...] = far_in[...].astype(BF16)

    @pl.when(far_seen)
    def _():
        def put(n, query_sum):
            dq[2 + n] += query_sum

        key_sum, value_sum = earlier_sums(FAR, (core, cross), kv_far, aux, put)
        far[:, :HD] = (far_in[:, :HD] + key_sum).astype(BF16)
        far[:, HD:] = (far_in[:, HD:] + value_sum).astype(BF16)


def kernel_call(kernel, name, out_shape, flops, *arrays):
    vmem = pl.BlockSpec(memory_space=pltpu.VMEM)
    return pl.pallas_call(
        kernel,
        out_shape=out_shape,
        in_specs=[vmem] * len(arrays),
        out_specs=(vmem,) * len(out_shape),
        name=name,
        compiler_params=pltpu.CompilerParams(vmem_limit_bytes=VMEM_LIMIT),
        cost_estimate=pl.CostEstimate(flops=flops, bytes_accessed=1 << 20, transcendentals=0),
    )(*arrays)


def own_kernel(msg, kv, aux, dq, dkv):
    blk = lax.axis_index("blk")
    threshold = aux[0:1, :] - (blk * ROWS).astype(F32)
    key_at = lax.broadcasted_iota(jnp.int32, (ROWS, ROWS), 0)
    query_at = lax.broadcasted_iota(jnp.int32, (ROWS, ROWS), 1)
    causal = both(jnp.where(key_at <= query_at, key_at, -1).astype(F32))

    def put(n, query_sum):
        dq[n] = query_sum

    key_sum, value_sum = sums_of(
        (msg,),
        kv[:, :HD],
        kv[:, HD:],
        both(aux[1:2, :] * SCALE),
        causal >= both(jnp.maximum(threshold, 0.0)),
        put,
    )
    dkv[:, :HD] = key_sum
    dkv[:, HD:] = value_sum


def turn_kernel(dq, send, keep):
    for n, (kept, sent) in enumerate(((0, 2), (1, 3))):
        at = slice(2 * n * ROWS, 2 * (n + 1) * ROWS)
        keep[at, :] = dq[kept].T
        send[at, :] = dq[sent].T.astype(BF16)


def query_kernel(dq_keep, dq_core, dq_y, grad_query):
    for h in range(2):
        at = slice(h * ROWS, (h + 1) * ROWS)
        total = dq_keep[at, :] + dq_core[at, :].astype(F32) + dq_y[at, :].astype(F32)
        grad_query[:, h * HD : (h + 1) * HD] = (total * SCALE).astype(BF16)


def terms_kernel(own, far, near, terms):
    share = terms.shape[1]
    for n, head in enumerate(HEAD_ORDER):
        at = slice(head * share, (head + 1) * share)
        total = own[at, :] + far[at, :].astype(F32) + near[at, :].astype(F32)
        terms[n] = total.astype(BF16)


def key_value_kernel(terms, grad_key, grad_value):
    for g in range(2):
        total = 0.0
        for n, head in enumerate(HEAD_ORDER):
            if head // 8 == g:
                total = total + terms[n].astype(F32)
        grad_key[:, g * HD : (g + 1) * HD] = (total[:, :HD] * SCALE).astype(BF16)
        grad_value[:, g * HD : (g + 1) * HD] = total[:, HD:].astype(BF16)


def local(
    query,
    key,
    value,
    output,
    grad_output,
    log_norm,
    entropy,
    segment_ids,
    weight_index,
    penalty_weights,
):
    to_core = pairs_from(other_core)
    to_y = pairs_from(other_y)
    back_near = pairs_from(functools.partial(back_source, NEAR))
    back_far = pairs_from(functools.partial(back_source, FAR))
    msg, kv, aux = prep(
        query,
        key,
        value,
        output,
        grad_output,
        log_norm,
        entropy,
        segment_ids.reshape(-1, HD),
        weight_index,
        penalty_weights,
    )
    kv_near = moved(kv, back_near)
    msg_y = moved(msg, to_y)
    kv_far = moved(kv, back_far)
    msg_other = moved(jnp.concatenate([msg, msg_y], axis=0), to_core)
    sums = functools.partial(jax.ShapeDtypeStruct, dtype=F32)
    pair = jax.ShapeDtypeStruct((ROWS, 2 * HD), BF16)
    dq_own, dkv_own = kernel_call(
        own_kernel,
        "own",
        (sums((1, HD, 2 * ROWS)), sums((ROWS, 2 * HD))),
        OWN_FLOPS,
        msg,
        kv,
        aux,
    )
    dkv_far, dq = kernel_call(
        early_kernel,
        "early",
        (sums((ROWS, 2 * HD)), sums((2, HD, 2 * ROWS))),
        EARLY_FLOPS,
        msg,
        msg_y,
        kv_far,
        aux,
        dq_own,
    )
    dkv_far, dkv_near, dq = kernel_call(
        late_kernel,
        "late",
        (pair, pair, sums((4, HD, 2 * ROWS))),
        LATE_FLOPS,
        msg,
        msg_y,
        kv_near,
        kv_far,
        msg_other,
        aux,
        dkv_far,
        dq,
    )
    got_near = moved(dkv_near, inverse(back_near))
    got_far = moved(dkv_far, inverse(back_far))
    dq_send, dq_keep = kernel_call(
        turn_kernel,
        "turn",
        (jax.ShapeDtypeStruct((4 * ROWS, HD), BF16), sums((4 * ROWS, HD))),
        TURN_FLOPS,
        dq,
    )
    dq_core = moved(dq_send, to_core)
    dq_pass = (dq_keep[512:] + dq_core[512:].astype(F32)).astype(BF16)
    share = jax.ShapeDtypeStruct((16, ROWS // 16, 2 * HD), BF16)
    (terms,) = kernel_call(terms_kernel, "terms", (share,), 0, dkv_own, got_far, got_near)
    dq_y = moved(dq_pass, to_y)
    terms = lax.all_to_all(terms, "head", 0, 0, axis_index_groups=[HEAD_ORDER])
    (grad_query,) = kernel_call(query_kernel, "query", (pair,), QUERY_FLOPS, dq_keep, dq_core, dq_y)
    result = jax.ShapeDtypeStruct((terms.shape[1], 2 * HD), BF16)
    return (grad_query, *kernel_call(key_value_kernel, "key_value", (result, result), 0, terms))


def solution(mesh):
    in_specs = (
        P("blk", "head"),
        P("blk", None),
        P("blk", None),
        P("blk", "head"),
        P("blk", "head"),
        P("head", "blk"),
        P("head", "blk"),
        P(),
        P(),
        P(),
    )
    out_specs = (P("blk", "head"), P(("blk", "head"), None), P(("blk", "head"), None))
    return jax.shard_map(local, mesh=mesh, in_specs=in_specs, out_specs=out_specs, check_vma=False)
```

```python
import functools
import math

import jax
import jax.numpy as jnp
from jax import lax
from jax.experimental import pallas as pl
from jax.experimental.pallas import tpu as pltpu
from jax.sharding import PartitionSpec as P

HD = 128
ROWS = 256
SCALE = HD ** (-0.5)
LOG2E = math.log2(math.e)
MSG = 4 * ROWS + 64
GROUP = 8
F32 = jnp.float32
OWN_FLOPS = 1 << 28
EARLY_FLOPS = 1 << 34
LATE_FLOPS = 1 << 30
QUERY_FLOPS = 1 << 27
PART_FLOPS = 1 << 34
TERMS_FLOPS = 1 << 34
BF16 = jnp.bfloat16
VMEM_LIMIT = 24 * 1024 * 1024

NEAR = ((1, 7), (2, 6))
FAR = ((3, 5), (4, 8))

HEAD_ORDER = [y * 4 + z_hi * 2 + core for z_hi in (1, 0) for y in range(4) for core in range(2)]


def place(index):
    blk, head = divmod(index, 16)
    x, z_lo = divmod(blk, 8)
    y, rest = divmod(head, 4)
    z_hi, core = divmod(rest, 2)
    return x, y, z_hi * 8 + z_lo, core


def device(x, y, z, core):
    z_hi, z_lo = divmod(z % 16, 8)
    return ((x % 4) * 8 + z_lo) * 16 + (y % 4) * 4 + z_hi * 2 + core


def pairs_from(source_of):
    return [(source_of(index), index) for index in range(512)]


def back_source(table, index):
    x, y, z, core = place(index)
    steps = table[y % 2][core]
    source_x = x if z % 8 >= steps else x - 1
    up = steps < 4 or (steps == 4 and z % 2 == 0)
    return device(source_x, y, z - steps if up else z + 8 - steps, core)


def other_core(index):
    x, y, z, core = place(index)
    return device(x, y, z, 1 - core)


def other_y(index):
    x, y, z, core = place(index)
    return device(x, y ^ 1, z, core)


def inverse(pairs):
    return [(target, source) for source, target in pairs]


def moved(value, pairs):
    return lax.ppermute(value, ("blk", "head"), pairs)


def steps_here(table):
    head = lax.axis_index("head")
    odd = lax.rem(lax.div(head, 4), 2) == 1
    core = lax.rem(head, 2) == 1
    return jnp.where(
        odd,
        jnp.where(core, table[1][1], table[1][0]),
        jnp.where(core, table[0][1], table[0][0]),
    )


def nt(a, b):
    return lax.dot_general(a, b, (((1,), (1,)), ((), ())), preferred_element_type=F32)


def nn(a, b):
    return lax.dot_general(a, b, (((1,), (0,)), ((), ())), preferred_element_type=F32)


def transposed(block):
    return block.astype(F32).T.astype(BF16)


def prep_kernel(
    q_in,
    k_in,
    v_in,
    o_in,
    do_in,
    lse_in,
    ent_in,
    seg_in,
    weight_index_in,
    weights_in,
    msg,
    kv,
    aux,
    q,
    k,
    v,
    o,
    do,
    lse,
    ent,
    seg,
    weight_index,
    weights,
    rows,
    sems,
):
    arriving = [
        pltpu.make_async_copy(source, target, sems.at[n])
        for n, (source, target) in enumerate(
            (
                (weight_index_in, weight_index),
                (weights_in, weights),
                (seg_in, seg),
                (lse_in, lse),
                (ent_in, ent),
                (do_in, do),
                (o_in, o),
                (q_in, q),
                (k_in, k),
                (v_in, v),
            )
        )
    ]
    for copy in arriving:
        copy.start()
    for copy in arriving:
        copy.wait()
    blk = lax.axis_index("blk")
    head = lax.axis_index("head")
    column = pl.multiple_of(lax.div(head, 8) * HD, HD)
    kv[:, :HD] = k[:, pl.ds(column, HD)]
    kv[:, HD:] = v[:, pl.ds(column, HD)]
    docs = weight_index.shape[0]
    tokens = seg[...]
    first = seg[pl.ds(2 * blk, 1), :]
    second = seg[pl.ds(2 * blk + 1, 1), :]
    seg_rows = jnp.concatenate([first, second], axis=1)
    rate = jnp.zeros((1, ROWS), F32)
    for d in range(docs):
        rows[d : d + 1, :HD] = jnp.sum(
            jnp.where(tokens < d, 1.0, 0.0), axis=0, keepdims=True
        )
        rate = jnp.where(seg_rows == d, weights[weight_index[d]], rate)
    starts = jnp.sum(rows[:docs, :HD], axis=1, keepdims=True)
    doc = lax.broadcasted_iota(jnp.int32, (docs, ROWS), 0)
    start = jnp.sum(jnp.where(doc == seg_rows, starts, 0.0), axis=0, keepdims=True)
    aux[...] = jnp.zeros_like(aux)
    aux[0:1, :] = start
    aux[1:2, :] = rate
    rows[...] = jnp.zeros_like(rows)
    for h in range(2):
        columns = slice(h * HD, (h + 1) * HD)
        do_h = do[:, columns]
        msg[h * ROWS : (h + 1) * ROWS, :] = q[:, columns]
        msg[(2 + h) * ROWS : (3 + h) * ROWS, :] = do_h
        product = do_h.astype(F32) * o[:, columns].astype(F32)
        delta = jnp.sum(product.T, axis=0, keepdims=True)
        lse_h = lse[h : h + 1, :]
        const = delta + rate * (ent[h : h + 1, :] - lse_h)
        for at, value in ((0, lse_h), (3, const)):
            for part in range(3):
                piece = value.astype(BF16).astype(F32)
                rows[at + part : at + part + 1, :] = piece
                value = value - piece
        at = 1024 + 32 * h
        msg[at : at + 16, :] = rows[:, :HD].astype(BF16)
        msg[at + 16 : at + 32, :] = rows[:, HD:].astype(BF16)


def prep(*arrays):
    vmem = pl.BlockSpec(memory_space=pltpu.VMEM)
    held = [pltpu.VMEM(array.shape, array.dtype) for array in arrays[:8]]
    held += [pltpu.SMEM(array.shape, array.dtype) for array in arrays[8:]]
    return pl.pallas_call(
        prep_kernel,
        out_shape=(
            jax.ShapeDtypeStruct((MSG, HD), BF16),
            jax.ShapeDtypeStruct((ROWS, 2 * HD), BF16),
            jax.ShapeDtypeStruct((8, ROWS), F32),
        ),
        in_specs=[pl.BlockSpec(memory_space=pltpu.HBM)] * 10,
        out_specs=(vmem,) * 3,
        scratch_shapes=held
        + [pltpu.VMEM((16, ROWS), F32), pltpu.SemaphoreType.DMA((10,))],
        name="prep",
        compiler_params=pltpu.CompilerParams(vmem_limit_bytes=VMEM_LIMIT),
    )(*[pltpu.with_memory_space_constraint(array, pltpu.HBM) for array in arrays])


def both(row):
    return jnp.concatenate([row, row], axis=1)


def row_terms(msg):
    halves = [msg[at : at + 16, :].astype(F32) for at in range(4 * ROWS, MSG, 16)]

    def whole(row):
        return jnp.concatenate(
            [
                half[row : row + 1, :] + half[row + 1 : row + 2, :] + half[row + 2 : row + 3, :]
                for half in halves
            ],
            axis=1,
        )

    return whole(0) * LOG2E, whole(3)


def probs_and_dscores(key_block, value_block, msg, rate, visible):
    lse2, const = row_terms(msg)
    scores = nt(key_block, msg[: 2 * ROWS, :])
    probs = jnp.where(visible, jnp.exp2(scores * (SCALE * LOG2E) - lse2), 0.0)
    dprobs = nt(value_block, msg[2 * ROWS : 4 * ROWS, :])
    dscores = probs * (dprobs - const - scores * rate)
    return probs.astype(BF16), dscores.astype(BF16)


def sums_of(messages, key_block, value_block, rate, visible, put_query_sum):
    key_turned = transposed(key_block)
    key_sum = value_sum = before = None
    for n, msg in enumerate((*messages, None)):
        here = None
        if msg is not None:
            here = probs_and_dscores(key_block, value_block, msg, rate, visible)
        if before is not None:
            probs, dscores = before
            past = messages[n - 1]
            put_query_sum(n - 1, nn(key_turned, dscores))
            key_add = nn(dscores, past[: 2 * ROWS, :])
            value_add = nn(probs, past[2 * ROWS : 4 * ROWS, :])
            key_sum = key_add if key_sum is None else key_sum + key_add
            value_sum = value_add if value_sum is None else value_sum + value_add
        before = here
    return key_sum, value_sum


def block_place(table, start):
    key_start = ((lax.axis_index("blk") - steps_here(table)) * ROWS).astype(F32)
    return start - key_start, key_start + (ROWS - 1) >= jnp.min(start)


def earlier_sums(table, messages, kv, aux, put):
    reach, _ = block_place(table, aux[0:1, :])
    key_at = lax.broadcasted_iota(jnp.int32, (ROWS, 2 * ROWS), 0).astype(F32)
    return sums_of(
        messages,
        kv[:, :HD],
        kv[:, HD:],
        both(aux[1:2, :] * SCALE),
        key_at >= both(reach),
        put,
    )


def early_kernel(own, y, kv_far, aux, far, dq):
    _, seen = block_place(FAR, aux[0:1, :])

    @pl.when(jnp.logical_not(seen))
    def _():
        dq[...] = jnp.zeros_like(dq)
        far[...] = jnp.zeros_like(far)

    @pl.when(seen)
    def _():
        def put(n, query_sum):
            dq[n] = query_sum

        key_sum, value_sum = earlier_sums(FAR, (own, y), kv_far, aux, put)
        far[:, :HD] = key_sum
        far[:, HD:] = value_sum


def late_kernel(own, y, kv_near, kv_far, other, aux, far_in, dq_in, far, near, dq):
    core, cross = other.at[:MSG, :], other.at[MSG:, :]
    _, far_seen = block_place(FAR, aux[0:1, :])
    _, near_seen = block_place(NEAR, aux[0:1, :])

    @pl.when(jnp.logical_not(near_seen))
    def _():
        dq[:2] = dq_in[...]
        dq[2:] = jnp.zeros_like(dq[2:])
        near[...] = jnp.zeros_like(near)

    @pl.when(near_seen)
    def _():
        def put(n, query_sum):
            dq[n] = dq_in[n] + query_sum if n < 2 else query_sum

        key_sum, value_sum = earlier_sums(NEAR, (own, y, core, cross), kv_near, aux, put)
        near[:, :HD] = key_sum.astype(BF16)
        near[:, HD:] = value_sum.astype(BF16)

    @pl.when(jnp.logical_not(far_seen))
    def _():
        far[...] = far_in[...].astype(BF16)

    @pl.when(far_seen)
    def _():
        def put(n, query_sum):
            dq[2 + n] += query_sum

        key_sum, value_sum = earlier_sums(FAR, (core, cross), kv_far, aux, put)
        far[:, :HD] = (far_in[:, :HD] + key_sum).astype(BF16)
        far[:, HD:] = (far_in[:, HD:] + value_sum).astype(BF16)


def kernel_call(kernel, name, out_shape, flops, *arrays):
    vmem = pl.BlockSpec(memory_space=pltpu.VMEM)
    return pl.pallas_call(
        kernel,
        out_shape=out_shape,
        in_specs=[vmem] * len(arrays),
        out_specs=(vmem,) * len(out_shape),
        name=name,
        compiler_params=pltpu.CompilerParams(vmem_limit_bytes=VMEM_LIMIT),
        cost_estimate=pl.CostEstimate(flops=flops, bytes_accessed=1 << 20, transcendentals=0),
    )(*arrays)


def own_kernel(msg, kv, aux, dq, dkv, keep, core, send):
    blk = lax.axis_index("blk")
    threshold = aux[0:1, :] - (blk * ROWS).astype(F32)
    key_at = lax.broadcasted_iota(jnp.int32, (ROWS, ROWS), 0)
    query_at = lax.broadcasted_iota(jnp.int32, (ROWS, ROWS), 1)
    causal = both(jnp.where(key_at <= query_at, key_at, -1).astype(F32))

    def put(n, query_sum):
        keep[...] = (dq[0] + query_sum).T

    key_sum, value_sum = sums_of(
        (msg,),
        kv[:, :HD],
        kv[:, HD:],
        both(aux[1:2, :] * SCALE),
        causal >= both(jnp.maximum(threshold, 0.0)),
        put,
    )
    dkv[:, :HD] = key_sum
    dkv[:, HD:] = value_sum
    core[...] = dq[2].T
    send[: 2 * ROWS, :] = dq[1].T.astype(BF16)
    send[2 * ROWS :, :] = dq[3].T.astype(BF16)


def part_kernel(keep, core, dq_y, part, onward):
    part[...] = keep[...] + dq_y[: 2 * ROWS, :].astype(F32)
    onward[...] = (core[...] + dq_y[2 * ROWS :, :].astype(F32)).astype(BF16)


def query_kernel(part, dq_core, grad_query):
    for h in range(2):
        at = slice(h * ROWS, (h + 1) * ROWS)
        total = part[at, :] + dq_core[at, :].astype(F32)
        grad_query[:, h * HD : (h + 1) * HD] = (total * SCALE).astype(BF16)


def terms_kernel(own, far, near, terms):
    share = terms.shape[1]
    for n, head in enumerate(HEAD_ORDER):
        at = slice(head * share, (head + 1) * share)
        total = own[at, :] + far[at, :].astype(F32) + near[at, :].astype(F32)
        terms[n] = total.astype(BF16)


def key_value_kernel(terms, grad_key, grad_value):
    for g in range(2):
        total = 0.0
        for n, head in enumerate(HEAD_ORDER):
            if head // 8 == g:
                total = total + terms[n].astype(F32)
        grad_key[:, g * HD : (g + 1) * HD] = (total[:, :HD] * SCALE).astype(BF16)
        grad_value[:, g * HD : (g + 1) * HD] = total[:, HD:].astype(BF16)


def local(
    query,
    key,
    value,
    output,
    grad_output,
    log_norm,
    entropy,
    segment_ids,
    weight_index,
    penalty_weights,
):
    to_core = pairs_from(other_core)
    to_y = pairs_from(other_y)
    back_near = pairs_from(functools.partial(back_source, NEAR))
    back_far = pairs_from(functools.partial(back_source, FAR))
    msg, kv, aux = prep(
        query,
        key,
        value,
        output,
        grad_output,
        log_norm,
        entropy,
        segment_ids.reshape(-1, HD),
        weight_index,
        penalty_weights,
    )
    kv_near = moved(kv, back_near)
    msg_y = moved(msg, to_y)
    kv_far = moved(kv, back_far)
    msg_other = moved(jnp.concatenate([msg, msg_y], axis=0), to_core)
    sums = functools.partial(jax.ShapeDtypeStruct, dtype=F32)
    pair = jax.ShapeDtypeStruct((ROWS, 2 * HD), BF16)
    dkv_far, dq = kernel_call(
        early_kernel,
        "early",
        (sums((ROWS, 2 * HD)), sums((2, HD, 2 * ROWS))),
        EARLY_FLOPS,
        msg,
        msg_y,
        kv_far,
        aux,
    )
    dkv_far, dkv_near, dq = kernel_call(
        late_kernel,
        "late",
        (pair, pair, sums((4, HD, 2 * ROWS))),
        LATE_FLOPS,
        msg,
        msg_y,
        kv_near,
        kv_far,
        msg_other,
        aux,
        dkv_far,
        dq,
    )
    got_near = moved(dkv_near, inverse(back_near))
    got_far = moved(dkv_far, inverse(back_far))
    held = sums((2 * ROWS, HD))
    dkv_own, dq_keep, dq_core, dq_y = kernel_call(
        own_kernel,
        "own",
        (sums((ROWS, 2 * HD)), held, held, jax.ShapeDtypeStruct((4 * ROWS, HD), BF16)),
        OWN_FLOPS,
        msg,
        kv,
        aux,
        dq,
    )
    dq_y = moved(dq_y, to_y)
    dq_part, dq_core = kernel_call(
        part_kernel,
        "part",
        (held, jax.ShapeDtypeStruct((2 * ROWS, HD), BF16)),
        PART_FLOPS,
        dq_keep,
        dq_core,
        dq_y,
    )
    dq_core = moved(dq_core, to_core)
    share = jax.ShapeDtypeStruct((16, ROWS // 16, 2 * HD), BF16)
    (terms,) = kernel_call(terms_kernel, "terms", (share,), TERMS_FLOPS, dkv_own, got_far, got_near)
    terms = lax.all_to_all(terms, "head", 0, 0, axis_index_groups=[HEAD_ORDER])
    (grad_query,) = kernel_call(query_kernel, "query", (pair,), QUERY_FLOPS, dq_part, dq_core)
    result = jax.ShapeDtypeStruct((terms.shape[1], 2 * HD), BF16)
    return (grad_query, *kernel_call(key_value_kernel, "key_value", (result, result), 0, terms))


def solution(mesh):
    in_specs = (
        P("blk", "head"),
        P("blk", None),
        P("blk", None),
        P("blk", "head"),
        P("blk", "head"),
        P("head", "blk"),
        P("head", "blk"),
        P(),
        P(),
        P(),
    )
    out_specs = (P("blk", "head"), P(("blk", "head"), None), P(("blk", "head"), None))
    return jax.shard_map(local, mesh=mesh, in_specs=in_specs, out_specs=out_specs, check_vma=False)
```

```python
import functools
import math

import jax
import jax.numpy as jnp
from jax import lax
from jax.experimental import pallas as pl
from jax.experimental.pallas import tpu as pltpu
from jax.sharding import PartitionSpec as P

HD = 128
ROWS = 256
SCALE = HD ** (-0.5)
LOG2E = math.log2(math.e)
MSG = 4 * ROWS + 64
GROUP = 8
F32 = jnp.float32
OWN_FLOPS = 1 << 28
EARLY_FLOPS = 1 << 34
LATE_FLOPS = 1 << 30
QUERY_FLOPS = 1 << 27
PART_FLOPS = 1 << 34
TERMS_FLOPS = 1 << 34
BF16 = jnp.bfloat16
VMEM_LIMIT = 24 * 1024 * 1024

NEAR = ((1, 7), (8, 2))
FAR = ((5, 3), (4, 6))

HEAD_ORDER = [y * 4 + z_hi * 2 + core for z_hi in (1, 0) for y in range(4) for core in range(2)]


def place(index):
    blk, head = divmod(index, 16)
    x, z_lo = divmod(blk, 8)
    y, rest = divmod(head, 4)
    z_hi, core = divmod(rest, 2)
    return x, y, z_hi * 8 + z_lo, core


def device(x, y, z, core):
    z_hi, z_lo = divmod(z % 16, 8)
    return ((x % 4) * 8 + z_lo) * 16 + (y % 4) * 4 + z_hi * 2 + core


def pairs_from(source_of):
    return [(source_of(index), index) for index in range(512)]


def back_source(table, index):
    x, y, z, core = place(index)
    steps = table[y % 2][core]
    source_x = x if z % 8 >= steps else x - 1
    up = steps < 4 or (steps == 4 and z % 4 != 3)
    return device(source_x, y, z - steps if up else z + 8 - steps, core)


def other_core(index):
    x, y, z, core = place(index)
    return device(x, y, z, 1 - core)


def other_y(index):
    x, y, z, core = place(index)
    return device(x, y ^ 1, z, core)


def inverse(pairs):
    return [(target, source) for source, target in pairs]


def moved(value, pairs):
    return lax.ppermute(value, ("blk", "head"), pairs)


def steps_here(table):
    head = lax.axis_index("head")
    odd = lax.rem(lax.div(head, 4), 2) == 1
    core = lax.rem(head, 2) == 1
    return jnp.where(
        odd,
        jnp.where(core, table[1][1], table[1][0]),
        jnp.where(core, table[0][1], table[0][0]),
    )


def nt(a, b):
    return lax.dot_general(a, b, (((1,), (1,)), ((), ())), preferred_element_type=F32)


def nn(a, b):
    return lax.dot_general(a, b, (((1,), (0,)), ((), ())), preferred_element_type=F32)


def transposed(block):
    return block.astype(F32).T.astype(BF16)


def prep_kernel(
    q_in,
    k_in,
    v_in,
    o_in,
    do_in,
    lse_in,
    ent_in,
    seg_in,
    weight_index_in,
    weights_in,
    msg,
    kv,
    aux,
    o,
    lse,
    ent,
    seg,
    weight_index,
    weights,
    rows,
    sems,
):
    blk = lax.axis_index("blk")
    column = pl.multiple_of(lax.div(lax.axis_index("head"), 8) * HD, HD)
    moves = [(weight_index_in, weight_index), (weights_in, weights), (seg_in, seg)]
    moves += [(lse_in, lse), (ent_in, ent), (o_in, o)]
    for first, source in ((2, do_in), (0, q_in)):
        for h in range(2):
            target = msg.at[(first + h) * ROWS : (first + h + 1) * ROWS, :]
            moves.append((source.at[:, h * HD : (h + 1) * HD], target))
    moves.append((k_in.at[:, pl.ds(column, HD)], kv.at[:, :HD]))
    moves.append((v_in.at[:, pl.ds(column, HD)], kv.at[:, HD:]))
    copies = [
        pltpu.make_async_copy(source, target, sems.at[n])
        for n, (source, target) in enumerate(moves)
    ]
    for copy in copies:
        copy.start()
    for copy in copies[:3]:
        copy.wait()
    docs = weight_index.shape[0]
    tokens = seg[...]
    first = seg[pl.ds(2 * blk, 1), :]
    second = seg[pl.ds(2 * blk + 1, 1), :]
    seg_rows = jnp.concatenate([first, second], axis=1)
    rate = jnp.zeros((1, ROWS), F32)
    for d in range(docs):
        rows[d : d + 1, :HD] = jnp.sum(
            jnp.where(tokens < d, 1.0, 0.0), axis=0, keepdims=True
        )
        rate = jnp.where(seg_rows == d, weights[weight_index[d]], rate)
    starts = jnp.sum(rows[:docs, :HD], axis=1, keepdims=True)
    doc = lax.broadcasted_iota(jnp.int32, (docs, ROWS), 0)
    start = jnp.sum(jnp.where(doc == seg_rows, starts, 0.0), axis=0, keepdims=True)
    aux[...] = jnp.zeros_like(aux)
    aux[0:1, :] = start
    aux[1:2, :] = rate
    rows[...] = jnp.zeros_like(rows)
    for copy in copies[3:8]:
        copy.wait()
    for h in range(2):
        do = msg[(2 + h) * ROWS : (3 + h) * ROWS, :]
        product = do.astype(F32) * o[:, h * HD : (h + 1) * HD].astype(F32)
        delta = jnp.sum(product.T, axis=0, keepdims=True)
        lse_h = lse[h : h + 1, :]
        const = delta + rate * (ent[h : h + 1, :] - lse_h)
        for at, value in ((0, lse_h), (3, const)):
            for part in range(3):
                piece = value.astype(BF16).astype(F32)
                rows[at + part : at + part + 1, :] = piece
                value = value - piece
        at = 1024 + 32 * h
        msg[at : at + 16, :] = rows[:, :HD].astype(BF16)
        msg[at + 16 : at + 32, :] = rows[:, HD:].astype(BF16)
    for copy in copies[8:]:
        copy.wait()


def prep(*arrays):
    vmem = pl.BlockSpec(memory_space=pltpu.VMEM)
    held = [pltpu.VMEM(arrays[n].shape, arrays[n].dtype) for n in (3, 5, 6, 7)]
    held += [pltpu.SMEM(array.shape, array.dtype) for array in arrays[8:]]
    return pl.pallas_call(
        prep_kernel,
        out_shape=(
            jax.ShapeDtypeStruct((MSG, HD), BF16),
            jax.ShapeDtypeStruct((ROWS, 2 * HD), BF16),
            jax.ShapeDtypeStruct((8, ROWS), F32),
        ),
        in_specs=[pl.BlockSpec(memory_space=pltpu.HBM)] * 10,
        out_specs=(vmem,) * 3,
        scratch_shapes=held
        + [pltpu.VMEM((16, ROWS), F32), pltpu.SemaphoreType.DMA((12,))],
        name="prep",
        compiler_params=pltpu.CompilerParams(vmem_limit_bytes=VMEM_LIMIT),
    )(*[pltpu.with_memory_space_constraint(array, pltpu.HBM) for array in arrays])


def both(row):
    return jnp.concatenate([row, row], axis=1)


def row_terms(msg):
    halves = [msg[at : at + 16, :].astype(F32) for at in range(4 * ROWS, MSG, 16)]

    def whole(row):
        return jnp.concatenate(
            [
                half[row : row + 1, :] + half[row + 1 : row + 2, :] + half[row + 2 : row + 3, :]
                for half in halves
            ],
            axis=1,
        )

    return whole(0) * LOG2E, whole(3)


def probs_and_dscores(key_block, value_block, msg, rate, visible):
    lse2, const = row_terms(msg)
    scores = nt(key_block, msg[: 2 * ROWS, :])
    probs = jnp.where(visible, jnp.exp2(scores * (SCALE * LOG2E) - lse2), 0.0)
    dprobs = nt(value_block, msg[2 * ROWS : 4 * ROWS, :])
    dscores = probs * (dprobs - const - scores * rate)
    return probs.astype(BF16), dscores.astype(BF16)


def sums_of(messages, key_block, value_block, rate, visible, put_query_sum):
    key_turned = transposed(key_block)
    key_sum = value_sum = before = None
    for n, msg in enumerate((*messages, None)):
        here = None
        if msg is not None:
            here = probs_and_dscores(key_block, value_block, msg, rate, visible)
        if before is not None:
            probs, dscores = before
            past = messages[n - 1]
            put_query_sum(n - 1, nn(key_turned, dscores))
            key_add = nn(dscores, past[: 2 * ROWS, :])
            value_add = nn(probs, past[2 * ROWS : 4 * ROWS, :])
            key_sum = key_add if key_sum is None else key_sum + key_add
            value_sum = value_add if value_sum is None else value_sum + value_add
        before = here
    return key_sum, value_sum


def block_place(table, start):
    key_start = ((lax.axis_index("blk") - steps_here(table)) * ROWS).astype(F32)
    return start - key_start, key_start + (ROWS - 1) >= jnp.min(start)


def earlier_sums(table, messages, kv, aux, put):
    reach, _ = block_place(table, aux[0:1, :])
    key_at = lax.broadcasted_iota(jnp.int32, (ROWS, 2 * ROWS), 0).astype(F32)
    return sums_of(
        messages,
        kv[:, :HD],
        kv[:, HD:],
        both(aux[1:2, :] * SCALE),
        key_at >= both(reach),
        put,
    )


def early_kernel(own, y, kv_far, aux, far, dq):
    _, seen = block_place(FAR, aux[0:1, :])

    @pl.when(jnp.logical_not(seen))
    def _():
        dq[...] = jnp.zeros_like(dq)
        far[...] = jnp.zeros_like(far)

    @pl.when(seen)
    def _():
        def put(n, query_sum):
            dq[n] = query_sum

        key_sum, value_sum = earlier_sums(FAR, (own, y), kv_far, aux, put)
        far[:, :HD] = key_sum
        far[:, HD:] = value_sum


def late_kernel(own, y, kv_near, kv_far, other, aux, far_in, dq_in, far, near, dq):
    core, cross = other.at[:MSG, :], other.at[MSG:, :]
    _, far_seen = block_place(FAR, aux[0:1, :])
    _, near_seen = block_place(NEAR, aux[0:1, :])

    @pl.when(jnp.logical_not(near_seen))
    def _():
        dq[:2] = dq_in[...]
        dq[2:] = jnp.zeros_like(dq[2:])
        near[...] = jnp.zeros_like(near)

    @pl.when(near_seen)
    def _():
        def put(n, query_sum):
            dq[n] = dq_in[n] + query_sum if n < 2 else query_sum

        key_sum, value_sum = earlier_sums(NEAR, (own, y, core, cross), kv_near, aux, put)
        near[:, :HD] = key_sum.astype(BF16)
        near[:, HD:] = value_sum.astype(BF16)

    @pl.when(jnp.logical_not(far_seen))
    def _():
        far[...] = far_in[...].astype(BF16)

    @pl.when(far_seen)
    def _():
        def put(n, query_sum):
            dq[2 + n] += query_sum

        key_sum, value_sum = earlier_sums(FAR, (core, cross), kv_far, aux, put)
        far[:, :HD] = (far_in[:, :HD] + key_sum).astype(BF16)
        far[:, HD:] = (far_in[:, HD:] + value_sum).astype(BF16)


def kernel_call(kernel, name, out_shape, flops, *arrays):
    vmem = pl.BlockSpec(memory_space=pltpu.VMEM)
    return pl.pallas_call(
        kernel,
        out_shape=out_shape,
        in_specs=[vmem] * len(arrays),
        out_specs=(vmem,) * len(out_shape),
        name=name,
        compiler_params=pltpu.CompilerParams(vmem_limit_bytes=VMEM_LIMIT),
        cost_estimate=pl.CostEstimate(flops=flops, bytes_accessed=1 << 20, transcendentals=0),
    )(*arrays)


def own_kernel(msg, kv, aux, dq, dkv, keep, core, send):
    blk = lax.axis_index("blk")
    threshold = aux[0:1, :] - (blk * ROWS).astype(F32)
    key_at = lax.broadcasted_iota(jnp.int32, (ROWS, ROWS), 0)
    query_at = lax.broadcasted_iota(jnp.int32, (ROWS, ROWS), 1)
    causal = both(jnp.where(key_at <= query_at, key_at, -1).astype(F32))

    def put(n, query_sum):
        keep[...] = (dq[0] + query_sum).T

    key_sum, value_sum = sums_of(
        (msg,),
        kv[:, :HD],
        kv[:, HD:],
        both(aux[1:2, :] * SCALE),
        causal >= both(jnp.maximum(threshold, 0.0)),
        put,
    )
    dkv[:, :HD] = key_sum
    dkv[:, HD:] = value_sum
    core[...] = dq[2].T
    send[: 2 * ROWS, :] = dq[1].T.astype(BF16)
    send[2 * ROWS :, :] = dq[3].T.astype(BF16)


def part_kernel(keep, core, dq_y, part, onward):
    part[...] = keep[...] + dq_y[: 2 * ROWS, :].astype(F32)
    onward[...] = (core[...] + dq_y[2 * ROWS :, :].astype(F32)).astype(BF16)


def query_kernel(part, dq_core, grad_query):
    for h in range(2):
        at = slice(h * ROWS, (h + 1) * ROWS)
        total = part[at, :] + dq_core[at, :].astype(F32)
        grad_query[:, h * HD : (h + 1) * HD] = (total * SCALE).astype(BF16)


def terms_kernel(own, far, near, terms):
    share = terms.shape[1]
    for n, head in enumerate(HEAD_ORDER):
        at = slice(head * share, (head + 1) * share)
        total = own[at, :] + far[at, :].astype(F32) + near[at, :].astype(F32)
        terms[n] = total.astype(BF16)


def key_value_kernel(terms, grad_key, grad_value):
    for g in range(2):
        total = 0.0
        for n, head in enumerate(HEAD_ORDER):
            if head // 8 == g:
                total = total + terms[n].astype(F32)
        grad_key[:, g * HD : (g + 1) * HD] = (total[:, :HD] * SCALE).astype(BF16)
        grad_value[:, g * HD : (g + 1) * HD] = total[:, HD:].astype(BF16)


def local(
    query,
    key,
    value,
    output,
    grad_output,
    log_norm,
    entropy,
    segment_ids,
    weight_index,
    penalty_weights,
):
    to_core = pairs_from(other_core)
    to_y = pairs_from(other_y)
    back_near = pairs_from(functools.partial(back_source, NEAR))
    back_far = pairs_from(functools.partial(back_source, FAR))
    msg, kv, aux = prep(
        query,
        key,
        value,
        output,
        grad_output,
        log_norm,
        entropy,
        segment_ids.reshape(-1, HD),
        weight_index,
        penalty_weights,
    )
    kv_near = moved(kv, back_near)
    msg_y = moved(msg, to_y)
    kv_far = moved(kv, back_far)
    msg_other = moved(jnp.concatenate([msg, msg_y], axis=0), to_core)
    sums = functools.partial(jax.ShapeDtypeStruct, dtype=F32)
    pair = jax.ShapeDtypeStruct((ROWS, 2 * HD), BF16)
    dkv_far, dq = kernel_call(
        early_kernel,
        "early",
        (sums((ROWS, 2 * HD)), sums((2, HD, 2 * ROWS))),
        EARLY_FLOPS,
        msg,
        msg_y,
        kv_far,
        aux,
    )
    dkv_far, dkv_near, dq = kernel_call(
        late_kernel,
        "late",
        (pair, pair, sums((4, HD, 2 * ROWS))),
        LATE_FLOPS,
        msg,
        msg_y,
        kv_near,
        kv_far,
        msg_other,
        aux,
        dkv_far,
        dq,
    )
    got_near = moved(dkv_near, inverse(back_near))
    got_far = moved(dkv_far, inverse(back_far))
    held = sums((2 * ROWS, HD))
    dkv_own, dq_keep, dq_core, dq_y = kernel_call(
        own_kernel,
        "own",
        (sums((ROWS, 2 * HD)), held, held, jax.ShapeDtypeStruct((4 * ROWS, HD), BF16)),
        OWN_FLOPS,
        msg,
        kv,
        aux,
        dq,
    )
    dq_y = moved(dq_y, to_y)
    dq_part, dq_core = kernel_call(
        part_kernel,
        "part",
        (held, jax.ShapeDtypeStruct((2 * ROWS, HD), BF16)),
        PART_FLOPS,
        dq_keep,
        dq_core,
        dq_y,
    )
    dq_core = moved(dq_core, to_core)
    share = jax.ShapeDtypeStruct((16, ROWS // 16, 2 * HD), BF16)
    (terms,) = kernel_call(terms_kernel, "terms", (share,), TERMS_FLOPS, dkv_own, got_far, got_near)
    terms = lax.all_to_all(terms, "head", 0, 0, axis_index_groups=[HEAD_ORDER])
    (grad_query,) = kernel_call(query_kernel, "query", (pair,), QUERY_FLOPS, dq_part, dq_core)
    result = jax.ShapeDtypeStruct((terms.shape[1], 2 * HD), BF16)
    return (grad_query, *kernel_call(key_value_kernel, "key_value", (result, result), 0, terms))


def solution(mesh):
    in_specs = (
        P("blk", "head"),
        P("blk", None),
        P("blk", None),
        P("blk", "head"),
        P("blk", "head"),
        P("head", "blk"),
        P("head", "blk"),
        P(),
        P(),
        P(),
    )
    out_specs = (P("blk", "head"), P(("blk", "head"), None), P(("blk", "head"), None))
    return jax.shard_map(local, mesh=mesh, in_specs=in_specs, out_specs=out_specs, check_vma=False)
```

```python
import functools
import math

import jax
import jax.numpy as jnp
from jax import lax
from jax.experimental import pallas as pl
from jax.experimental.pallas import tpu as pltpu
from jax.sharding import PartitionSpec as P

HD = 128
ROWS = 256
SCALE = HD ** (-0.5)
LOG2E = math.log2(math.e)
MSG = 4 * ROWS + 64
GROUP = 8
F32 = jnp.float32
OWN_FLOPS = 1 << 28
EARLY_FLOPS = 1 << 34
LATE_FLOPS = 1 << 30
QUERY_FLOPS = 1 << 27
PART_FLOPS = 1 << 34
TERMS_FLOPS = 1 << 34
BF16 = jnp.bfloat16
VMEM_LIMIT = 24 * 1024 * 1024

NEAR = ((1, 7), (8, 2))
FAR = ((5, 3), (4, 6))

HEAD_ORDER = [y * 4 + z_hi * 2 + core for z_hi in (1, 0) for y in range(4) for core in range(2)]


def place(index):
    blk, head = divmod(index, 16)
    x, z_lo = divmod(blk, 8)
    y, rest = divmod(head, 4)
    z_hi, core = divmod(rest, 2)
    return x, y, z_hi * 8 + z_lo, core


def device(x, y, z, core):
    z_hi, z_lo = divmod(z % 16, 8)
    return ((x % 4) * 8 + z_lo) * 16 + (y % 4) * 4 + z_hi * 2 + core


def pairs_from(source_of):
    return [(source_of(index), index) for index in range(512)]


def back_source(table, index):
    x, y, z, core = place(index)
    steps = table[y % 2][core]
    source_x = x if z % 8 >= steps else x - 1
    up = steps < 4 or (steps == 4 and z % 2 == 0)
    return device(source_x, y, z - steps if up else z + 8 - steps, core)


def other_core(index):
    x, y, z, core = place(index)
    return device(x, y, z, 1 - core)


def other_y(index):
    x, y, z, core = place(index)
    return device(x, y ^ 1, z, core)


def inverse(pairs):
    return [(target, source) for source, target in pairs]


def moved(value, pairs):
    return lax.ppermute(value, ("blk", "head"), pairs)


def steps_here(table):
    head = lax.axis_index("head")
    odd = lax.rem(lax.div(head, 4), 2) == 1
    core = lax.rem(head, 2) == 1
    return jnp.where(
        odd,
        jnp.where(core, table[1][1], table[1][0]),
        jnp.where(core, table[0][1], table[0][0]),
    )


def nt(a, b):
    return lax.dot_general(a, b, (((1,), (1,)), ((), ())), preferred_element_type=F32)


def nn(a, b):
    return lax.dot_general(a, b, (((1,), (0,)), ((), ())), preferred_element_type=F32)


def transposed(block):
    return block.astype(F32).T.astype(BF16)


def prep_kernel(
    q_in,
    k_in,
    v_in,
    o_in,
    do_in,
    lse_in,
    ent_in,
    seg_in,
    weight_index_in,
    weights_in,
    msg,
    kv,
    aux,
    o,
    lse,
    ent,
    seg,
    weight_index,
    weights,
    rows,
    sems,
):
    blk = lax.axis_index("blk")
    column = pl.multiple_of(lax.div(lax.axis_index("head"), 8) * HD, HD)
    moves = [(weight_index_in, weight_index), (weights_in, weights), (seg_in, seg)]
    moves += [(lse_in, lse), (ent_in, ent), (o_in, o)]
    for first, source in ((2, do_in), (0, q_in)):
        for h in range(2):
            target = msg.at[(first + h) * ROWS : (first + h + 1) * ROWS, :]
            moves.append((source.at[:, h * HD : (h + 1) * HD], target))
    moves.append((k_in.at[:, pl.ds(column, HD)], kv.at[:, :HD]))
    moves.append((v_in.at[:, pl.ds(column, HD)], kv.at[:, HD:]))
    copies = [
        pltpu.make_async_copy(source, target, sems.at[n])
        for n, (source, target) in enumerate(moves)
    ]
    for copy in copies:
        copy.start()
    for copy in copies[:3]:
        copy.wait()
    docs = weight_index.shape[0]
    tokens = seg[...]
    first = seg[pl.ds(2 * blk, 1), :]
    second = seg[pl.ds(2 * blk + 1, 1), :]
    seg_rows = jnp.concatenate([first, second], axis=1)
    rate = jnp.zeros((1, ROWS), F32)
    for d in range(docs):
        rows[d : d + 1, :HD] = jnp.sum(
            jnp.where(tokens < d, 1.0, 0.0), axis=0, keepdims=True
        )
        rate = jnp.where(seg_rows == d, weights[weight_index[d]], rate)
    starts = jnp.sum(rows[:docs, :HD], axis=1, keepdims=True)
    doc = lax.broadcasted_iota(jnp.int32, (docs, ROWS), 0)
    start = jnp.sum(jnp.where(doc == seg_rows, starts, 0.0), axis=0, keepdims=True)
    aux[...] = jnp.zeros_like(aux)
    aux[0:1, :] = start
    aux[1:2, :] = rate
    rows[...] = jnp.zeros_like(rows)
    for copy in copies[3:8]:
        copy.wait()
    for h in range(2):
        do = msg[(2 + h) * ROWS : (3 + h) * ROWS, :]
        product = do.astype(F32) * o[:, h * HD : (h + 1) * HD].astype(F32)
        delta = jnp.sum(product.T, axis=0, keepdims=True)
        lse_h = lse[h : h + 1, :]
        const = delta + rate * (ent[h : h + 1, :] - lse_h)
        for at, value in ((0, lse_h), (3, const)):
            for part in range(3):
                piece = value.astype(BF16).astype(F32)
                rows[at + part : at + part + 1, :] = piece
                value = value - piece
        at = 1024 + 32 * h
        msg[at : at + 16, :] = rows[:, :HD].astype(BF16)
        msg[at + 16 : at + 32, :] = rows[:, HD:].astype(BF16)
    for copy in copies[8:]:
        copy.wait()


def prep(*arrays):
    vmem = pl.BlockSpec(memory_space=pltpu.VMEM)
    held = [pltpu.VMEM(arrays[n].shape, arrays[n].dtype) for n in (3, 5, 6, 7)]
    held += [pltpu.SMEM(array.shape, array.dtype) for array in arrays[8:]]
    return pl.pallas_call(
        prep_kernel,
        out_shape=(
            jax.ShapeDtypeStruct((MSG, HD), BF16),
            jax.ShapeDtypeStruct((ROWS, 2 * HD), BF16),
            jax.ShapeDtypeStruct((8, ROWS), F32),
        ),
        in_specs=[pl.BlockSpec(memory_space=pltpu.HBM)] * 10,
        out_specs=(vmem,) * 3,
        scratch_shapes=held
        + [pltpu.VMEM((16, ROWS), F32), pltpu.SemaphoreType.DMA((12,))],
        name="prep",
        compiler_params=pltpu.CompilerParams(vmem_limit_bytes=VMEM_LIMIT),
    )(*[pltpu.with_memory_space_constraint(array, pltpu.HBM) for array in arrays])


def both(row):
    return jnp.concatenate([row, row], axis=1)


def row_terms(msg):
    halves = [msg[at : at + 16, :].astype(F32) for at in range(4 * ROWS, MSG, 16)]

    def whole(row):
        return jnp.concatenate(
            [
                half[row : row + 1, :] + half[row + 1 : row + 2, :] + half[row + 2 : row + 3, :]
                for half in halves
            ],
            axis=1,
        )

    return whole(0) * LOG2E, whole(3)


def probs_and_dscores(key_block, value_block, msg, rate, visible):
    lse2, const = row_terms(msg)
    scores = nt(key_block, msg[: 2 * ROWS, :])
    probs = jnp.where(visible, jnp.exp2(scores * (SCALE * LOG2E) - lse2), 0.0)
    dprobs = nt(value_block, msg[2 * ROWS : 4 * ROWS, :])
    dscores = probs * (dprobs - const - scores * rate)
    return probs.astype(BF16), dscores.astype(BF16)


def sums_of(messages, key_block, value_block, rate, visible, put_query_sum):
    key_turned = transposed(key_block)
    key_sum = value_sum = before = None
    for n, msg in enumerate((*messages, None)):
        here = None
        if msg is not None:
            here = probs_and_dscores(key_block, value_block, msg, rate, visible)
        if before is not None:
            probs, dscores = before
            past = messages[n - 1]
            put_query_sum(n - 1, nn(key_turned, dscores))
            key_add = nn(dscores, past[: 2 * ROWS, :])
            value_add = nn(probs, past[2 * ROWS : 4 * ROWS, :])
            key_sum = key_add if key_sum is None else key_sum + key_add
            value_sum = value_add if value_sum is None else value_sum + value_add
        before = here
    return key_sum, value_sum


def block_place(table, start):
    key_start = ((lax.axis_index("blk") - steps_here(table)) * ROWS).astype(F32)
    return start - key_start, key_start + (ROWS - 1) >= jnp.min(start)


def earlier_sums(table, messages, kv, aux, put):
    reach, _ = block_place(table, aux[0:1, :])
    key_at = lax.broadcasted_iota(jnp.int32, (ROWS, 2 * ROWS), 0).astype(F32)
    return sums_of(
        messages,
        kv[:, :HD],
        kv[:, HD:],
        both(aux[1:2, :] * SCALE),
        key_at >= both(reach),
        put,
    )


def early_kernel(own, y, kv_far, aux, far, dq):
    _, seen = block_place(FAR, aux[0:1, :])

    @pl.when(jnp.logical_not(seen))
    def _():
        dq[...] = jnp.zeros_like(dq)
        far[...] = jnp.zeros_like(far)

    @pl.when(seen)
    def _():
        def put(n, query_sum):
            dq[n] = query_sum

        key_sum, value_sum = earlier_sums(FAR, (own, y), kv_far, aux, put)
        far[:, :HD] = key_sum
        far[:, HD:] = value_sum


def late_kernel(own, y, kv_near, kv_far, other, aux, far_in, dq_in, far, near, dq):
    core, cross = other.at[:MSG, :], other.at[MSG:, :]
    _, far_seen = block_place(FAR, aux[0:1, :])
    _, near_seen = block_place(NEAR, aux[0:1, :])

    @pl.when(jnp.logical_not(near_seen))
    def _():
        dq[:2] = dq_in[...]
        dq[2:] = jnp.zeros_like(dq[2:])
        near[...] = jnp.zeros_like(near)

    @pl.when(near_seen)
    def _():
        def put(n, query_sum):
            dq[n] = dq_in[n] + query_sum if n < 2 else query_sum

        key_sum, value_sum = earlier_sums(NEAR, (own, y, core, cross), kv_near, aux, put)
        near[:, :HD] = key_sum.astype(BF16)
        near[:, HD:] = value_sum.astype(BF16)

    @pl.when(jnp.logical_not(far_seen))
    def _():
        far[...] = far_in[...].astype(BF16)

    @pl.when(far_seen)
    def _():
        def put(n, query_sum):
            dq[2 + n] += query_sum

        key_sum, value_sum = earlier_sums(FAR, (core, cross), kv_far, aux, put)
        far[:, :HD] = (far_in[:, :HD] + key_sum).astype(BF16)
        far[:, HD:] = (far_in[:, HD:] + value_sum).astype(BF16)


def kernel_call(kernel, name, out_shape, flops, *arrays):
    vmem = pl.BlockSpec(memory_space=pltpu.VMEM)
    return pl.pallas_call(
        kernel,
        out_shape=out_shape,
        in_specs=[vmem] * len(arrays),
        out_specs=(vmem,) * len(out_shape),
        name=name,
        compiler_params=pltpu.CompilerParams(vmem_limit_bytes=VMEM_LIMIT),
        cost_estimate=pl.CostEstimate(flops=flops, bytes_accessed=1 << 20, transcendentals=0),
    )(*arrays)


def own_kernel(msg, kv, aux, dq, dkv, keep, core, send):
    blk = lax.axis_index("blk")
    threshold = aux[0:1, :] - (blk * ROWS).astype(F32)
    key_at = lax.broadcasted_iota(jnp.int32, (ROWS, ROWS), 0)
    query_at = lax.broadcasted_iota(jnp.int32, (ROWS, ROWS), 1)
    causal = both(jnp.where(key_at <= query_at, key_at, -1).astype(F32))

    def put(n, query_sum):
        keep[...] = (dq[0] + query_sum).T

    key_sum, value_sum = sums_of(
        (msg,),
        kv[:, :HD],
        kv[:, HD:],
        both(aux[1:2, :] * SCALE),
        causal >= both(jnp.maximum(threshold, 0.0)),
        put,
    )
    dkv[:, :HD] = key_sum
    dkv[:, HD:] = value_sum
    core[...] = dq[2].T
    send[: 2 * ROWS, :] = dq[1].T.astype(BF16)
    send[2 * ROWS :, :] = dq[3].T.astype(BF16)


def part_kernel(keep, core, dq_y, part, onward):
    part[...] = keep[...] + dq_y[: 2 * ROWS, :].astype(F32)
    onward[...] = (core[...] + dq_y[2 * ROWS :, :].astype(F32)).astype(BF16)


def query_kernel(part, dq_core, grad_query):
    for h in range(2):
        at = slice(h * ROWS, (h + 1) * ROWS)
        total = part[at, :] + dq_core[at, :].astype(F32)
        grad_query[:, h * HD : (h + 1) * HD] = (total * SCALE).astype(BF16)


def terms_kernel(own, far, near, terms):
    share = terms.shape[1]
    for n, head in enumerate(HEAD_ORDER):
        at = slice(head * share, (head + 1) * share)
        total = own[at, :] + far[at, :].astype(F32) + near[at, :].astype(F32)
        terms[n] = total.astype(BF16)


def key_value_kernel(terms, grad_key, grad_value):
    for g in range(2):
        total = 0.0
        for n, head in enumerate(HEAD_ORDER):
            if head // 8 == g:
                total = total + terms[n].astype(F32)
        grad_key[:, g * HD : (g + 1) * HD] = (total[:, :HD] * SCALE).astype(BF16)
        grad_value[:, g * HD : (g + 1) * HD] = total[:, HD:].astype(BF16)


def local(
    query,
    key,
    value,
    output,
    grad_output,
    log_norm,
    entropy,
    segment_ids,
    weight_index,
    penalty_weights,
):
    to_core = pairs_from(other_core)
    to_y = pairs_from(other_y)
    back_near = pairs_from(functools.partial(back_source, NEAR))
    back_far = pairs_from(functools.partial(back_source, FAR))
    msg, kv, aux = prep(
        query,
        key,
        value,
        output,
        grad_output,
        log_norm,
        entropy,
        segment_ids.reshape(-1, HD),
        weight_index,
        penalty_weights,
    )
    kv_near = moved(kv, back_near)
    msg_y = moved(msg, to_y)
    kv_far = moved(kv, back_far)
    msg_other = moved(jnp.concatenate([msg, msg_y], axis=0), to_core)
    sums = functools.partial(jax.ShapeDtypeStruct, dtype=F32)
    pair = jax.ShapeDtypeStruct((ROWS, 2 * HD), BF16)
    dkv_far, dq = kernel_call(
        early_kernel,
        "early",
        (sums((ROWS, 2 * HD)), sums((2, HD, 2 * ROWS))),
        EARLY_FLOPS,
        msg,
        msg_y,
        kv_far,
        aux,
    )
    dkv_far, dkv_near, dq = kernel_call(
        late_kernel,
        "late",
        (pair, pair, sums((4, HD, 2 * ROWS))),
        LATE_FLOPS,
        msg,
        msg_y,
        kv_near,
        kv_far,
        msg_other,
        aux,
        dkv_far,
        dq,
    )
    got_near = moved(dkv_near, inverse(back_near))
    got_far = moved(dkv_far, inverse(back_far))
    held = sums((2 * ROWS, HD))
    dkv_own, dq_keep, dq_core, dq_y = kernel_call(
        own_kernel,
        "own",
        (sums((ROWS, 2 * HD)), held, held, jax.ShapeDtypeStruct((4 * ROWS, HD), BF16)),
        OWN_FLOPS,
        msg,
        kv,
        aux,
        dq,
    )
    dq_y = moved(dq_y, to_y)
    dq_part, dq_core = kernel_call(
        part_kernel,
        "part",
        (held, jax.ShapeDtypeStruct((2 * ROWS, HD), BF16)),
        PART_FLOPS,
        dq_keep,
        dq_core,
        dq_y,
    )
    dq_core = moved(dq_core, to_core)
    share = jax.ShapeDtypeStruct((16, ROWS // 16, 2 * HD), BF16)
    (terms,) = kernel_call(terms_kernel, "terms", (share,), TERMS_FLOPS, dkv_own, got_far, got_near)
    terms = lax.all_to_all(terms, "head", 0, 0, axis_index_groups=[HEAD_ORDER])
    (grad_query,) = kernel_call(query_kernel, "query", (pair,), QUERY_FLOPS, dq_part, dq_core)
    result = jax.ShapeDtypeStruct((terms.shape[1], 2 * HD), BF16)
    return (grad_query, *kernel_call(key_value_kernel, "key_value", (result, result), 0, terms))


def solution(mesh):
    in_specs = (
        P("blk", "head"),
        P("blk", None),
        P("blk", None),
        P("blk", "head"),
        P("blk", "head"),
        P("head", "blk"),
        P("head", "blk"),
        P(),
        P(),
        P(),
    )
    out_specs = (P("blk", "head"), P(("blk", "head"), None), P(("blk", "head"), None))
    return jax.shard_map(local, mesh=mesh, in_specs=in_specs, out_specs=out_specs, check_vma=False)
```

```python
import functools
import math

import jax
import jax.numpy as jnp
from jax import lax
from jax.experimental import pallas as pl
from jax.experimental.pallas import tpu as pltpu
from jax.sharding import PartitionSpec as P

HD = 128
ROWS = 256
SCALE = HD ** (-0.5)
LOG2E = math.log2(math.e)
MSG = 4 * ROWS + 64
GROUP = 8
F32 = jnp.float32
OWN_FLOPS = 1 << 28
EARLY_FLOPS = 1 << 34
LATE_FLOPS = 1 << 30
QUERY_FLOPS = 1 << 27
PART_FLOPS = 1 << 34
TERMS_FLOPS = 1 << 34
BF16 = jnp.bfloat16
VMEM_LIMIT = 24 * 1024 * 1024

NEAR = ((1, 7), (8, 2))
FAR = ((5, 3), (4, 6))

HEAD_ORDER = [y * 4 + z_hi * 2 + core for z_hi in (1, 0) for y in range(4) for core in range(2)]


def place(index):
    blk, head = divmod(index, 16)
    x, z_lo = divmod(blk, 8)
    y, rest = divmod(head, 4)
    z_hi, core = divmod(rest, 2)
    return x, y, z_hi * 8 + z_lo, core


def device(x, y, z, core):
    z_hi, z_lo = divmod(z % 16, 8)
    return ((x % 4) * 8 + z_lo) * 16 + (y % 4) * 4 + z_hi * 2 + core


def pairs_from(source_of):
    return [(source_of(index), index) for index in range(512)]


def back_source(table, index):
    x, y, z, core = place(index)
    steps = table[y % 2][core]
    source_x = x if z % 8 >= steps else x - 1
    up = steps < 4 or (steps == 4 and z % 2 == 0)
    return device(source_x, y, z - steps if up else z + 8 - steps, core)


def other_core(index):
    x, y, z, core = place(index)
    return device(x, y, z, 1 - core)


def other_y(index):
    x, y, z, core = place(index)
    return device(x, y ^ 1, z, core)


def inverse(pairs):
    return [(target, source) for source, target in pairs]


def moved(value, pairs):
    return lax.ppermute(value, ("blk", "head"), pairs)


def steps_here(table):
    head = lax.axis_index("head")
    odd = lax.rem(lax.div(head, 4), 2) == 1
    core = lax.rem(head, 2) == 1
    return jnp.where(
        odd,
        jnp.where(core, table[1][1], table[1][0]),
        jnp.where(core, table[0][1], table[0][0]),
    )


def nt(a, b):
    return lax.dot_general(a, b, (((1,), (1,)), ((), ())), preferred_element_type=F32)


def nn(a, b):
    return lax.dot_general(a, b, (((1,), (0,)), ((), ())), preferred_element_type=F32)


def transposed(block):
    return block.astype(F32).T.astype(BF16)


def prep_kernel(
    q_in,
    k_in,
    v_in,
    o_in,
    do_in,
    lse_in,
    ent_in,
    seg_in,
    weight_index_in,
    weights_in,
    msg,
    kv,
    aux,
    o,
    lse,
    ent,
    seg,
    weight_index,
    weights,
    rows,
    sems,
):
    blk = lax.axis_index("blk")
    column = pl.multiple_of(lax.div(lax.axis_index("head"), 8) * HD, HD)
    moves = [(weight_index_in, weight_index), (weights_in, weights), (seg_in, seg)]
    moves += [(lse_in, lse), (ent_in, ent), (o_in, o)]
    for first, source in ((2, do_in), (0, q_in)):
        for h in range(2):
            target = msg.at[(first + h) * ROWS : (first + h + 1) * ROWS, :]
            moves.append((source.at[:, h * HD : (h + 1) * HD], target))
    moves.append((k_in.at[:, pl.ds(column, HD)], kv.at[:, :HD]))
    moves.append((v_in.at[:, pl.ds(column, HD)], kv.at[:, HD:]))
    copies = [
        pltpu.make_async_copy(source, target, sems.at[n])
        for n, (source, target) in enumerate(moves)
    ]
    for copy in copies:
        copy.start()
    for copy in copies[:3]:
        copy.wait()
    docs = weight_index.shape[0]
    tokens = seg[...]
    first = seg[pl.ds(2 * blk, 1), :]
    second = seg[pl.ds(2 * blk + 1, 1), :]
    seg_rows = jnp.concatenate([first, second], axis=1)
    rate = jnp.zeros((1, ROWS), F32)
    for d in range(docs):
        rows[d : d + 1, :HD] = jnp.sum(
            jnp.where(tokens < d, 1.0, 0.0), axis=0, keepdims=True
        )
        rate = jnp.where(seg_rows == d, weights[weight_index[d]], rate)
    starts = jnp.sum(rows[:docs, :HD], axis=1, keepdims=True)
    doc = lax.broadcasted_iota(jnp.int32, (docs, ROWS), 0)
    start = jnp.sum(jnp.where(doc == seg_rows, starts, 0.0), axis=0, keepdims=True)
    aux[...] = jnp.zeros_like(aux)
    aux[0:1, :] = start
    aux[1:2, :] = rate
    rows[...] = jnp.zeros_like(rows)
    for copy in copies[3:8]:
        copy.wait()
    for h in range(2):
        do = msg[(2 + h) * ROWS : (3 + h) * ROWS, :]
        product = do.astype(F32) * o[:, h * HD : (h + 1) * HD].astype(F32)
        delta = jnp.sum(product.T, axis=0, keepdims=True)
        lse_h = lse[h : h + 1, :]
        const = delta + rate * (ent[h : h + 1, :] - lse_h)
        for at, value in ((0, lse_h), (3, const)):
            for part in range(3):
                piece = value.astype(BF16).astype(F32)
                rows[at + part : at + part + 1, :] = piece
                value = value - piece
        at = 1024 + 32 * h
        msg[at : at + 16, :] = rows[:, :HD].astype(BF16)
        msg[at + 16 : at + 32, :] = rows[:, HD:].astype(BF16)
    for copy in copies[8:]:
        copy.wait()


def prep(*arrays):
    vmem = pl.BlockSpec(memory_space=pltpu.VMEM)
    held = [pltpu.VMEM(arrays[n].shape, arrays[n].dtype) for n in (3, 5, 6, 7)]
    held += [pltpu.SMEM(array.shape, array.dtype) for array in arrays[8:]]
    return pl.pallas_call(
        prep_kernel,
        out_shape=(
            jax.ShapeDtypeStruct((MSG, HD), BF16),
            jax.ShapeDtypeStruct((ROWS, 2 * HD), BF16),
            jax.ShapeDtypeStruct((8, ROWS), F32),
        ),
        in_specs=[pl.BlockSpec(memory_space=pltpu.HBM)] * 10,
        out_specs=(vmem,) * 3,
        scratch_shapes=held
        + [pltpu.VMEM((16, ROWS), F32), pltpu.SemaphoreType.DMA((12,))],
        name="prep",
        compiler_params=pltpu.CompilerParams(vmem_limit_bytes=VMEM_LIMIT),
    )(*[pltpu.with_memory_space_constraint(array, pltpu.HBM) for array in arrays])


def both(row):
    return jnp.concatenate([row, row], axis=1)


def row_terms(msg):
    halves = [msg[at : at + 16, :].astype(F32) for at in range(4 * ROWS, MSG, 16)]

    def whole(row):
        return jnp.concatenate(
            [
                half[row : row + 1, :] + half[row + 1 : row + 2, :] + half[row + 2 : row + 3, :]
                for half in halves
            ],
            axis=1,
        )

    return whole(0) * LOG2E, whole(3)


def probs_and_dscores(key_block, value_block, msg, rate, visible):
    lse2, const = row_terms(msg)
    scores = nt(key_block, msg[: 2 * ROWS, :])
    probs = jnp.exp2(scores * (SCALE * LOG2E) - lse2)
    if visible is not None:
        probs = jnp.where(visible, probs, 0.0)
    dprobs = nt(value_block, msg[2 * ROWS : 4 * ROWS, :])
    dscores = probs * (dprobs - const - scores * rate)
    return probs.astype(BF16), dscores.astype(BF16)


def sums_of(messages, key_block, value_block, rate, visible, put_query_sum):
    key_turned = transposed(key_block)
    key_sum = value_sum = before = None
    for n, msg in enumerate((*messages, None)):
        here = None
        if msg is not None:
            here = probs_and_dscores(key_block, value_block, msg, rate, visible)
        if before is not None:
            probs, dscores = before
            past = messages[n - 1]
            put_query_sum(n - 1, nn(key_turned, dscores))
            key_add = nn(dscores, past[: 2 * ROWS, :])
            value_add = nn(probs, past[2 * ROWS : 4 * ROWS, :])
            key_sum = key_add if key_sum is None else key_sum + key_add
            value_sum = value_add if value_sum is None else value_sum + value_add
        before = here
    return key_sum, value_sum


def block_place(table, start):
    key_start = ((lax.axis_index("blk") - steps_here(table)) * ROWS).astype(F32)
    return start - key_start, key_start + (ROWS - 1) >= jnp.min(start)


def earlier_sums(table, messages, kv, aux, put, put_sums):
    reach, seen = block_place(table, aux[0:1, :])
    whole = jnp.max(reach) <= 0.0

    def run(visible):
        rate = both(aux[1:2, :] * SCALE)
        put_sums(*sums_of(messages, kv[:, :HD], kv[:, HD:], rate, visible, put))

    @pl.when(seen & whole)
    def _():
        run(None)

    @pl.when(seen & jnp.logical_not(whole))
    def _():
        key_at = lax.broadcasted_iota(jnp.int32, (ROWS, 2 * ROWS), 0).astype(F32)
        run(key_at >= both(reach))


def early_kernel(own, y, kv_far, aux, far, dq):
    _, seen = block_place(FAR, aux[0:1, :])

    @pl.when(jnp.logical_not(seen))
    def _():
        dq[...] = jnp.zeros_like(dq)
        far[...] = jnp.zeros_like(far)

    def put(n, query_sum):
        dq[n] = query_sum

    def put_sums(key_sum, value_sum):
        far[:, :HD] = key_sum
        far[:, HD:] = value_sum

    earlier_sums(FAR, (own, y), kv_far, aux, put, put_sums)


def late_kernel(own, y, kv_near, kv_far, other, aux, far_in, dq_in, far, near, dq):
    core, cross = other.at[:MSG, :], other.at[MSG:, :]
    _, far_seen = block_place(FAR, aux[0:1, :])
    _, near_seen = block_place(NEAR, aux[0:1, :])

    @pl.when(jnp.logical_not(near_seen))
    def _():
        dq[:2] = dq_in[...]
        dq[2:] = jnp.zeros_like(dq[2:])
        near[...] = jnp.zeros_like(near)

    def put_near(n, query_sum):
        dq[n] = dq_in[n] + query_sum if n < 2 else query_sum

    def put_near_sums(key_sum, value_sum):
        near[:, :HD] = key_sum.astype(BF16)
        near[:, HD:] = value_sum.astype(BF16)

    earlier_sums(NEAR, (own, y, core, cross), kv_near, aux, put_near, put_near_sums)

    @pl.when(jnp.logical_not(far_seen))
    def _():
        far[...] = far_in[...].astype(BF16)

    def put_far(n, query_sum):
        dq[2 + n] += query_sum

    def put_far_sums(key_sum, value_sum):
        far[:, :HD] = (far_in[:, :HD] + key_sum).astype(BF16)
        far[:, HD:] = (far_in[:, HD:] + value_sum).astype(BF16)

    earlier_sums(FAR, (core, cross), kv_far, aux, put_far, put_far_sums)


def kernel_call(kernel, name, out_shape, flops, *arrays):
    vmem = pl.BlockSpec(memory_space=pltpu.VMEM)
    return pl.pallas_call(
        kernel,
        out_shape=out_shape,
        in_specs=[vmem] * len(arrays),
        out_specs=(vmem,) * len(out_shape),
        name=name,
        compiler_params=pltpu.CompilerParams(vmem_limit_bytes=VMEM_LIMIT),
        cost_estimate=pl.CostEstimate(flops=flops, bytes_accessed=1 << 20, transcendentals=0),
    )(*arrays)


def own_kernel(msg, kv, aux, dq, dkv, keep, core, send):
    blk = lax.axis_index("blk")
    threshold = aux[0:1, :] - (blk * ROWS).astype(F32)
    key_at = lax.broadcasted_iota(jnp.int32, (ROWS, ROWS), 0)
    query_at = lax.broadcasted_iota(jnp.int32, (ROWS, ROWS), 1)
    causal = both(jnp.where(key_at <= query_at, key_at, -1).astype(F32))

    def put(n, query_sum):
        keep[...] = (dq[0] + query_sum).T

    key_sum, value_sum = sums_of(
        (msg,),
        kv[:, :HD],
        kv[:, HD:],
        both(aux[1:2, :] * SCALE),
        causal >= both(jnp.maximum(threshold, 0.0)),
        put,
    )
    dkv[:, :HD] = key_sum
    dkv[:, HD:] = value_sum
    core[...] = dq[2].T
    send[: 2 * ROWS, :] = dq[1].T.astype(BF16)
    send[2 * ROWS :, :] = dq[3].T.astype(BF16)


def part_kernel(keep, core, dq_y, part, onward):
    part[...] = keep[...] + dq_y[: 2 * ROWS, :].astype(F32)
    onward[...] = (core[...] + dq_y[2 * ROWS :, :].astype(F32)).astype(BF16)


def query_kernel(part, dq_core, grad_query):
    for h in range(2):
        at = slice(h * ROWS, (h + 1) * ROWS)
        total = part[at, :] + dq_core[at, :].astype(F32)
        grad_query[:, h * HD : (h + 1) * HD] = (total * SCALE).astype(BF16)


def terms_kernel(own, far, near, terms):
    share = terms.shape[1]
    for n, head in enumerate(HEAD_ORDER):
        at = slice(head * share, (head + 1) * share)
        total = own[at, :] + far[at, :].astype(F32) + near[at, :].astype(F32)
        terms[n] = total.astype(BF16)


def key_value_kernel(terms, grad_key, grad_value):
    for g in range(2):
        total = 0.0
        for n, head in enumerate(HEAD_ORDER):
            if head // 8 == g:
                total = total + terms[n].astype(F32)
        grad_key[:, g * HD : (g + 1) * HD] = (total[:, :HD] * SCALE).astype(BF16)
        grad_value[:, g * HD : (g + 1) * HD] = total[:, HD:].astype(BF16)


def local(
    query,
    key,
    value,
    output,
    grad_output,
    log_norm,
    entropy,
    segment_ids,
    weight_index,
    penalty_weights,
):
    to_core = pairs_from(other_core)
    to_y = pairs_from(other_y)
    back_near = pairs_from(functools.partial(back_source, NEAR))
    back_far = pairs_from(functools.partial(back_source, FAR))
    msg, kv, aux = prep(
        query,
        key,
        value,
        output,
        grad_output,
        log_norm,
        entropy,
        segment_ids.reshape(-1, HD),
        weight_index,
        penalty_weights,
    )
    kv_near = moved(kv, back_near)
    msg_y = moved(msg, to_y)
    kv_far = moved(kv, back_far)
    msg_other = moved(jnp.concatenate([msg, msg_y], axis=0), to_core)
    sums = functools.partial(jax.ShapeDtypeStruct, dtype=F32)
    pair = jax.ShapeDtypeStruct((ROWS, 2 * HD), BF16)
    dkv_far, dq = kernel_call(
        early_kernel,
        "early",
        (sums((ROWS, 2 * HD)), sums((2, HD, 2 * ROWS))),
        EARLY_FLOPS,
        msg,
        msg_y,
        kv_far,
        aux,
    )
    dkv_far, dkv_near, dq = kernel_call(
        late_kernel,
        "late",
        (pair, pair, sums((4, HD, 2 * ROWS))),
        LATE_FLOPS,
        msg,
        msg_y,
        kv_near,
        kv_far,
        msg_other,
        aux,
        dkv_far,
        dq,
    )
    got_near = moved(dkv_near, inverse(back_near))
    got_far = moved(dkv_far, inverse(back_far))
    held = sums((2 * ROWS, HD))
    dkv_own, dq_keep, dq_core, dq_y = kernel_call(
        own_kernel,
        "own",
        (sums((ROWS, 2 * HD)), held, held, jax.ShapeDtypeStruct((4 * ROWS, HD), BF16)),
        OWN_FLOPS,
        msg,
        kv,
        aux,
        dq,
    )
    dq_y = moved(dq_y, to_y)
    dq_part, dq_core = kernel_call(
        part_kernel,
        "part",
        (held, jax.ShapeDtypeStruct((2 * ROWS, HD), BF16)),
        PART_FLOPS,
        dq_keep,
        dq_core,
        dq_y,
    )
    dq_core = moved(dq_core, to_core)
    share = jax.ShapeDtypeStruct((16, ROWS // 16, 2 * HD), BF16)
    (terms,) = kernel_call(terms_kernel, "terms", (share,), TERMS_FLOPS, dkv_own, got_far, got_near)
    terms = lax.all_to_all(terms, "head", 0, 0, axis_index_groups=[HEAD_ORDER])
    (grad_query,) = kernel_call(query_kernel, "query", (pair,), QUERY_FLOPS, dq_part, dq_core)
    result = jax.ShapeDtypeStruct((terms.shape[1], 2 * HD), BF16)
    return (grad_query, *kernel_call(key_value_kernel, "key_value", (result, result), 0, terms))


def solution(mesh):
    in_specs = (
        P("blk", "head"),
        P("blk", None),
        P("blk", None),
        P("blk", "head"),
        P("blk", "head"),
        P("head", "blk"),
        P("head", "blk"),
        P(),
        P(),
        P(),
    )
    out_specs = (P("blk", "head"), P(("blk", "head"), None), P(("blk", "head"), None))
    return jax.shard_map(local, mesh=mesh, in_specs=in_specs, out_specs=out_specs, check_vma=False)
```

```python
import functools
import math

import jax
import jax.numpy as jnp
from jax import lax
from jax.experimental import pallas as pl
from jax.experimental.pallas import tpu as pltpu
from jax.sharding import PartitionSpec as P

HD = 128
ROWS = 256
SCALE = HD ** (-0.5)
LOG2E = math.log2(math.e)
MSG = 4 * ROWS + 64
GROUP = 8
F32 = jnp.float32
OWN_FLOPS = 1 << 28
EARLY_FLOPS = 1 << 34
LATE_FLOPS = 1 << 30
QUERY_FLOPS = 1 << 27
PART_FLOPS = 1 << 34
TERMS_FLOPS = 1 << 34
BF16 = jnp.bfloat16
VMEM_LIMIT = 24 * 1024 * 1024

NEAR = ((1, 7), (8, 2))
FAR = ((5, 3), (4, 6))

HEAD_ORDER = [y * 4 + z_hi * 2 + core for z_hi in (1, 0) for y in range(4) for core in range(2)]


def place(index):
    blk, head = divmod(index, 16)
    x, z_lo = divmod(blk, 8)
    y, rest = divmod(head, 4)
    z_hi, core = divmod(rest, 2)
    return x, y, z_hi * 8 + z_lo, core


def device(x, y, z, core):
    z_hi, z_lo = divmod(z % 16, 8)
    return ((x % 4) * 8 + z_lo) * 16 + (y % 4) * 4 + z_hi * 2 + core


def pairs_from(source_of):
    return [(source_of(index), index) for index in range(512)]


def back_source(table, index):
    x, y, z, core = place(index)
    steps = table[y % 2][core]
    source_x = x if z % 8 >= steps else x - 1
    up = steps < 4 or (steps == 4 and z % 2 == 0)
    return device(source_x, y, z - steps if up else z + 8 - steps, core)


def other_core(index):
    x, y, z, core = place(index)
    return device(x, y, z, 1 - core)


def other_y(index):
    x, y, z, core = place(index)
    return device(x, y ^ 1, z, core)


def inverse(pairs):
    return [(target, source) for source, target in pairs]


def moved(value, pairs):
    return lax.ppermute(value, ("blk", "head"), pairs)


def steps_here(table):
    head = lax.axis_index("head")
    odd = lax.rem(lax.div(head, 4), 2) == 1
    core = lax.rem(head, 2) == 1
    return jnp.where(
        odd,
        jnp.where(core, table[1][1], table[1][0]),
        jnp.where(core, table[0][1], table[0][0]),
    )


def nt(a, b):
    return lax.dot_general(a, b, (((1,), (1,)), ((), ())), preferred_element_type=F32)


def nn(a, b):
    return lax.dot_general(a, b, (((1,), (0,)), ((), ())), preferred_element_type=F32)


def transposed(block):
    return block.astype(F32).T.astype(BF16)


def prep_kernel(
    q_in,
    k_in,
    v_in,
    o_in,
    do_in,
    lse_in,
    ent_in,
    seg_in,
    weight_index_in,
    weights_in,
    msg,
    kv,
    aux,
    o,
    lse,
    ent,
    seg,
    weight_index,
    weights,
    rows,
    sems,
):
    blk = lax.axis_index("blk")
    column = pl.multiple_of(lax.div(lax.axis_index("head"), 8) * HD, HD)
    moves = [(weight_index_in, weight_index), (weights_in, weights), (seg_in, seg)]
    moves += [(lse_in, lse), (ent_in, ent), (o_in, o)]
    for first, source in ((2, do_in), (0, q_in)):
        for h in range(2):
            target = msg.at[(first + h) * ROWS : (first + h + 1) * ROWS, :]
            moves.append((source.at[:, h * HD : (h + 1) * HD], target))
    moves.append((k_in.at[:, pl.ds(column, HD)], kv.at[:, :HD]))
    moves.append((v_in.at[:, pl.ds(column, HD)], kv.at[:, HD:]))
    copies = [
        pltpu.make_async_copy(source, target, sems.at[n])
        for n, (source, target) in enumerate(moves)
    ]
    for copy in copies:
        copy.start()
    for copy in copies[:3]:
        copy.wait()
    docs = weight_index.shape[0]
    tokens = seg[...]
    first = seg[pl.ds(2 * blk, 1), :]
    second = seg[pl.ds(2 * blk + 1, 1), :]
    seg_rows = jnp.concatenate([first, second], axis=1)
    rate = jnp.zeros((1, ROWS), F32)
    for d in range(docs):
        rows[d : d + 1, :HD] = jnp.sum(
            jnp.where(tokens < d, 1.0, 0.0), axis=0, keepdims=True
        )
        rate = jnp.where(seg_rows == d, weights[weight_index[d]], rate)
    starts = jnp.sum(rows[:docs, :HD], axis=1, keepdims=True)
    doc = lax.broadcasted_iota(jnp.int32, (docs, ROWS), 0)
    start = jnp.sum(jnp.where(doc == seg_rows, starts, 0.0), axis=0, keepdims=True)
    aux[...] = jnp.zeros_like(aux)
    aux[0:1, :] = start
    aux[1:2, :] = rate
    rows[...] = jnp.zeros_like(rows)
    for copy in copies[3:8]:
        copy.wait()
    for h in range(2):
        do = msg[(2 + h) * ROWS : (3 + h) * ROWS, :]
        product = do.astype(F32) * o[:, h * HD : (h + 1) * HD].astype(F32)
        delta = jnp.sum(product.T, axis=0, keepdims=True)
        lse_h = lse[h : h + 1, :]
        const = delta + rate * (ent[h : h + 1, :] - lse_h)
        for at, value in ((0, lse_h), (3, const)):
            for part in range(3):
                piece = value.astype(BF16).astype(F32)
                rows[at + part : at + part + 1, :] = piece
                value = value - piece
        at = 1024 + 32 * h
        msg[at : at + 16, :] = rows[:, :HD].astype(BF16)
        msg[at + 16 : at + 32, :] = rows[:, HD:].astype(BF16)
    for copy in copies[8:]:
        copy.wait()


def prep(*arrays):
    vmem = pl.BlockSpec(memory_space=pltpu.VMEM)
    held = [pltpu.VMEM(arrays[n].shape, arrays[n].dtype) for n in (3, 5, 6, 7)]
    held += [pltpu.SMEM(array.shape, array.dtype) for array in arrays[8:]]
    return pl.pallas_call(
        prep_kernel,
        out_shape=(
            jax.ShapeDtypeStruct((MSG, HD), BF16),
            jax.ShapeDtypeStruct((ROWS, 2 * HD), BF16),
            jax.ShapeDtypeStruct((8, ROWS), F32),
        ),
        in_specs=[pl.BlockSpec(memory_space=pltpu.HBM)] * 10,
        out_specs=(vmem,) * 3,
        scratch_shapes=held
        + [pltpu.VMEM((16, ROWS), F32), pltpu.SemaphoreType.DMA((12,))],
        name="prep",
        compiler_params=pltpu.CompilerParams(vmem_limit_bytes=VMEM_LIMIT),
    )(*[pltpu.with_memory_space_constraint(array, pltpu.HBM) for array in arrays])


def both(row):
    return jnp.concatenate([row, row], axis=1)


def row_terms(msg):
    halves = [msg[at : at + 16, :].astype(F32) for at in range(4 * ROWS, MSG, 16)]

    def whole(row):
        return jnp.concatenate(
            [
                half[row : row + 1, :] + half[row + 1 : row + 2, :] + half[row + 2 : row + 3, :]
                for half in halves
            ],
            axis=1,
        )

    return whole(0) * LOG2E, whole(3)


def probs_and_dscores(key_block, value_block, msg, rate, visible):
    lse2, const = row_terms(msg)
    scores = nt(key_block, msg[: 2 * ROWS, :])
    probs = jnp.where(visible, jnp.exp2(scores * (SCALE * LOG2E) - lse2), 0.0)
    dprobs = nt(value_block, msg[2 * ROWS : 4 * ROWS, :])
    dscores = probs * (dprobs - const - scores * rate)
    return probs.astype(BF16), dscores.astype(BF16)


def sums_of(messages, key_block, value_block, rate, visible, put_query_sum):
    key_turned = transposed(key_block)
    key_sum = value_sum = before = None
    for n, msg in enumerate((*messages, None)):
        here = None
        if msg is not None:
            here = probs_and_dscores(key_block, value_block, msg, rate, visible)
        if before is not None:
            probs, dscores = before
            past = messages[n - 1]
            put_query_sum(n - 1, nn(key_turned, dscores))
            key_add = nn(dscores, past[: 2 * ROWS, :])
            value_add = nn(probs, past[2 * ROWS : 4 * ROWS, :])
            key_sum = key_add if key_sum is None else key_sum + key_add
            value_sum = value_add if value_sum is None else value_sum + value_add
        before = here
    return key_sum, value_sum


def block_place(table, start):
    key_start = ((lax.axis_index("blk") - steps_here(table)) * ROWS).astype(F32)
    return start - key_start, key_start + (ROWS - 1) >= jnp.min(start)


def earlier_sums(table, messages, kv, aux, put):
    reach, _ = block_place(table, aux[0:1, :])
    key_at = lax.broadcasted_iota(jnp.int32, (ROWS, 2 * ROWS), 0).astype(F32)
    return sums_of(
        messages,
        kv[:, :HD],
        kv[:, HD:],
        both(aux[1:2, :] * SCALE),
        key_at >= both(reach),
        put,
    )


def early_kernel(own, y, kv_far, aux, far, dq):
    _, seen = block_place(FAR, aux[0:1, :])

    @pl.when(jnp.logical_not(seen))
    def _():
        dq[...] = jnp.zeros_like(dq)
        far[...] = jnp.zeros_like(far)

    @pl.when(seen)
    def _():
        def put(n, query_sum):
            dq[n] = query_sum

        key_sum, value_sum = earlier_sums(FAR, (own, y), kv_far, aux, put)
        far[:, :HD] = key_sum
        far[:, HD:] = value_sum


def late_kernel(own, y, kv_near, kv_far, other, aux, far_in, dq_in, far, near, dq):
    core, cross = other.at[:MSG, :], other.at[MSG:, :]
    _, far_seen = block_place(FAR, aux[0:1, :])
    _, near_seen = block_place(NEAR, aux[0:1, :])

    @pl.when(jnp.logical_not(near_seen))
    def _():
        dq[:2] = dq_in[...]
        dq[2:] = jnp.zeros_like(dq[2:])
        near[...] = jnp.zeros_like(near)

    @pl.when(near_seen)
    def _():
        def put(n, query_sum):
            dq[n] = dq_in[n] + query_sum if n < 2 else query_sum

        key_sum, value_sum = earlier_sums(NEAR, (own, y, core, cross), kv_near, aux, put)
        near[:, :HD] = key_sum.astype(BF16)
        near[:, HD:] = value_sum.astype(BF16)

    @pl.when(jnp.logical_not(far_seen))
    def _():
        far[...] = far_in[...].astype(BF16)

    @pl.when(far_seen)
    def _():
        def put(n, query_sum):
            dq[2 + n] += query_sum

        key_sum, value_sum = earlier_sums(FAR, (core, cross), kv_far, aux, put)
        far[:, :HD] = (far_in[:, :HD] + key_sum).astype(BF16)
        far[:, HD:] = (far_in[:, HD:] + value_sum).astype(BF16)


def kernel_call(kernel, name, out_shape, flops, *arrays):
    vmem = pl.BlockSpec(memory_space=pltpu.VMEM)
    return pl.pallas_call(
        kernel,
        out_shape=out_shape,
        in_specs=[vmem] * len(arrays),
        out_specs=(vmem,) * len(out_shape),
        name=name,
        compiler_params=pltpu.CompilerParams(vmem_limit_bytes=VMEM_LIMIT),
        cost_estimate=pl.CostEstimate(flops=flops, bytes_accessed=1 << 20, transcendentals=0),
    )(*arrays)


def own_kernel(msg, kv, aux, dq, dkv, keep, core, send):
    blk = lax.axis_index("blk")
    threshold = aux[0:1, :] - (blk * ROWS).astype(F32)
    key_at = lax.broadcasted_iota(jnp.int32, (ROWS, ROWS), 0)
    query_at = lax.broadcasted_iota(jnp.int32, (ROWS, ROWS), 1)
    causal = both(jnp.where(key_at <= query_at, key_at, -1).astype(F32))

    def put(n, query_sum):
        keep[...] = (dq[0] + query_sum).T

    key_sum, value_sum = sums_of(
        (msg,),
        kv[:, :HD],
        kv[:, HD:],
        both(aux[1:2, :] * SCALE),
        causal >= both(jnp.maximum(threshold, 0.0)),
        put,
    )
    dkv[:, :HD] = key_sum
    dkv[:, HD:] = value_sum
    core[...] = dq[2].T
    send[: 2 * ROWS, :] = dq[1].T.astype(BF16)
    send[2 * ROWS :, :] = dq[3].T.astype(BF16)


def part_kernel(keep, core, dq_y, part, onward):
    part[...] = keep[...] + dq_y[: 2 * ROWS, :].astype(F32)
    onward[...] = (core[...] + dq_y[2 * ROWS :, :].astype(F32)).astype(BF16)


def query_kernel(part, dq_core, grad_query):
    for h in range(2):
        at = slice(h * ROWS, (h + 1) * ROWS)
        total = part[at, :] + dq_core[at, :].astype(F32)
        grad_query[:, h * HD : (h + 1) * HD] = (total * SCALE).astype(BF16)


def terms_kernel(own, near, far, terms):
    share = terms.shape[1]
    for n, head in enumerate(HEAD_ORDER):
        at = slice(head * share, (head + 1) * share)
        total = own[at, :] + far[at, :].astype(F32) + near[at, :].astype(F32)
        terms[n] = total.astype(BF16)


def key_value_kernel(terms, grad_key, grad_value):
    for g in range(2):
        total = 0.0
        for n, head in enumerate(HEAD_ORDER):
            if head // 8 == g:
                total = total + terms[n].astype(F32)
        grad_key[:, g * HD : (g + 1) * HD] = (total[:, :HD] * SCALE).astype(BF16)
        grad_value[:, g * HD : (g + 1) * HD] = total[:, HD:].astype(BF16)


def local(
    query,
    key,
    value,
    output,
    grad_output,
    log_norm,
    entropy,
    segment_ids,
    weight_index,
    penalty_weights,
):
    to_core = pairs_from(other_core)
    to_y = pairs_from(other_y)
    back_near = pairs_from(functools.partial(back_source, NEAR))
    back_far = pairs_from(functools.partial(back_source, FAR))
    msg, kv, aux = prep(
        query,
        key,
        value,
        output,
        grad_output,
        log_norm,
        entropy,
        segment_ids.reshape(-1, HD),
        weight_index,
        penalty_weights,
    )
    kv_near = moved(kv, back_near)
    msg_y = moved(msg, to_y)
    kv_far = moved(kv, back_far)
    msg_other = moved(jnp.concatenate([msg, msg_y], axis=0), to_core)
    sums = functools.partial(jax.ShapeDtypeStruct, dtype=F32)
    pair = jax.ShapeDtypeStruct((ROWS, 2 * HD), BF16)
    dkv_far, dq = kernel_call(
        early_kernel,
        "early",
        (sums((ROWS, 2 * HD)), sums((2, HD, 2 * ROWS))),
        EARLY_FLOPS,
        msg,
        msg_y,
        kv_far,
        aux,
    )
    dkv_far, dkv_near, dq = kernel_call(
        late_kernel,
        "late",
        (pair, pair, sums((4, HD, 2 * ROWS))),
        LATE_FLOPS,
        msg,
        msg_y,
        kv_near,
        kv_far,
        msg_other,
        aux,
        dkv_far,
        dq,
    )
    got_near = moved(dkv_near, inverse(back_near))
    got_far = moved(dkv_far, inverse(back_far))
    held = sums((2 * ROWS, HD))
    dkv_own, dq_keep, dq_core, dq_y = kernel_call(
        own_kernel,
        "own",
        (sums((ROWS, 2 * HD)), held, held, jax.ShapeDtypeStruct((4 * ROWS, HD), BF16)),
        OWN_FLOPS,
        msg,
        kv,
        aux,
        dq,
    )
    dq_y = moved(dq_y, to_y)
    dq_part, dq_core = kernel_call(
        part_kernel,
        "part",
        (held, jax.ShapeDtypeStruct((2 * ROWS, HD), BF16)),
        PART_FLOPS,
        dq_keep,
        dq_core,
        dq_y,
    )
    dq_core = moved(dq_core, to_core)
    share = jax.ShapeDtypeStruct((16, ROWS // 16, 2 * HD), BF16)
    (terms,) = kernel_call(terms_kernel, "terms", (share,), TERMS_FLOPS, dkv_own, got_near, got_far)
    terms = lax.all_to_all(terms, "head", 0, 0, axis_index_groups=[HEAD_ORDER])
    (grad_query,) = kernel_call(query_kernel, "query", (pair,), QUERY_FLOPS, dq_part, dq_core)
    result = jax.ShapeDtypeStruct((terms.shape[1], 2 * HD), BF16)
    return (grad_query, *kernel_call(key_value_kernel, "key_value", (result, result), 0, terms))


def solution(mesh):
    in_specs = (
        P("blk", "head"),
        P("blk", None),
        P("blk", None),
        P("blk", "head"),
        P("blk", "head"),
        P("head", "blk"),
        P("head", "blk"),
        P(),
        P(),
        P(),
    )
    out_specs = (P("blk", "head"), P(("blk", "head"), None), P(("blk", "head"), None))
    return jax.shard_map(local, mesh=mesh, in_specs=in_specs, out_specs=out_specs, check_vma=False)
```
